32 devices in a mesh: wide: 4 (over z), sec: 2 (over y), tile: 4 (over x, core).
Axes of the slice: x: 2, y: 2, z: 4, core: 2. Of those that a mesh axis runs over, the one named last changes fastest.
Arguments:
- velocity: float32 [3, 16, 64, 256], P(None, 'wide', 'tile', 'sec'), may hold values from -0.4 to 0.4
- viscosity: float32 [16, 64, 256], P('wide', 'tile', 'sec'), may hold values from 0.01 to 0.08
- counts: int32 [4, 2, 4], P('wide', 'sec', 'tile'), may hold values from 2 to 4, as said below
- destination: int32 [4, 2, 4, 4], P('wide', 'sec', 'tile'), may hold values from 0 to 3, as said below
- seeds: int32 [4, 2, 4, 4, 3, 128], P('wide', 'sec', 'tile'), may hold values from 0 to 127, as said below
- substeps: int32 [4, 2, 4, 4, 128], P('wide', 'sec', 'tile'), may hold values from 0 to 1
Outputs:
- new_velocity: float32 [3, 16, 64, 256], P(None, 'wide', 'tile', 'sec')
- traced_blocks: float32 [4, 2, 4, 8, 3, 128], P('wide', 'sec', 'tile')
The draws below stay inside these ranges and needn't reach their ends.
Inputs may be any that keep to these rules, and one draw needn't show every extreme that they name: Blocks 0 to counts - 1 of a device are live; some device has all 4 live. `destination`: among a device's live blocks at most 2 name any one tile, and exactly 2 name the tile that all devices with the same wide and sec index share. `seeds`: components 0, 1, 2 lie below 4, 16, 128.
All inputs are finite; a program needn't handle non-finite values.
Results may differ from the reference program's by a relative error of at most 0.0003.
Values sent between devices are 32-bit elements; how exact they have to be, the bound alone decides.
A program may use at most 64 MiB of HBM per device.

```python
import math
from functools import partial
import jax
import jax.numpy as jnp

CX = 4
CY = 16
CZ = 128
CAP = 2
PTS = 128
MAXSUB = 1
BLK_DEV = 4
SLOTS = 8
NX = 16
NY = 64
NZ = 256
N_WIDE = 4
N_SEC = 2
N_TILE = 4


def routing_table(key):
    key = jax.random.fold_in(key, 11)
    keys = jax.random.split(key, 6)
    shape = (N_WIDE, N_SEC, N_TILE)
    counts = jax.random.randint(keys[0], shape, CAP, BLK_DEV + 1)
    chosen = jax.random.randint(keys[1], (), 0, N_WIDE * N_SEC * N_TILE)
    flat_ids = jnp.arange(N_WIDE * N_SEC * N_TILE, dtype=jnp.int32).reshape(shape)
    counts = jnp.where(flat_ids == chosen, BLK_DEV, counts).astype(jnp.int32)
    hottest = jax.random.randint(keys[2], (N_WIDE, N_SEC, 1, 1), 0, N_TILE)
    block_ids = jnp.arange(BLK_DEV, dtype=jnp.int32)
    others = jnp.mod(hottest + 1 + jax.random.randint(keys[3], shape + (BLK_DEV,), 0, N_TILE - 1), N_TILE)
    filler = jax.random.randint(keys[4], shape + (BLK_DEV,), 0, N_TILE)
    counted = counts[..., None]
    ranked = jnp.where(block_ids < CAP, hottest, jnp.where(block_ids < counted, others, filler))
    scores = jax.random.randint(keys[5], shape + (BLK_DEV,), 0, 1 << 20) * BLK_DEV + block_ids
    scores = jnp.where(block_ids < counted, scores, (1 << 26) + block_ids)
    permuted = jnp.argsort(scores, axis=-1, stable=True)
    chosen_dest = jnp.take_along_axis(ranked, permuted, -1).astype(jnp.int32)
    return (counts, chosen_dest)


def draw_counts(key, part):
    return routing_table(key)[0]


def draw_destination(key, part):
    return routing_table(key)[1]


def draw_seeds(key, part):
    key = jax.random.fold_in(key, 23)
    upper_bound = jnp.array([CX, CY, CZ], jnp.int32).reshape(3, 1)
    return jax.random.randint(key, (N_WIDE, N_SEC, N_TILE, BLK_DEV, 3, PTS), 0, upper_bound).astype(jnp.int32)


def set_ends(values, rng, least, high):
    shape = values.shape
    index_at = [jax.random.randint(jax.random.fold_in(rng, axis), (), 0, shape[axis]) for axis in range(len(shape))]
    values = values.at[tuple(index_at)].set(least)
    longest = shape.index(max(shape))
    index_at[longest] = (index_at[longest] + 1) % shape[longest]
    return values.at[tuple(index_at)].set(high)


def steps_of(own_key, extent, shards, least, largest):
    def one(dim, shards_of):
        draws = jax.random.uniform(jax.random.fold_in(jax.random.fold_in(own_key, 6), dim), (shards_of,), jnp.float32, least / len(shards), largest / len(shards))
        return jnp.repeat(jnp.exp(draws), extent[dim] // shards_of).reshape((-1,) + (1,) * (len(extent) - dim - 1))

    loudness = one(*shards[0])
    for cut in shards[1:]:
        loudness = loudness * one(*cut)
    return loudness


def setup_inputs(seed: int = 0) -> dict:
    streams_of = jax.random.split(jax.random.key(seed), 7)
    velocity = jnp.clip(jax.random.uniform(streams_of[0], (3, NX, NY, NZ), jnp.float32, -0.4, 0.4) * steps_of(streams_of[0], (3, NX, NY, NZ), ((1, 4), (2, 4), (3, 2)), -0.4, 0.0), -0.4, 0.4)
    viscosity = jnp.clip(jnp.exp(math.log(0.08) - 2.0794415 * jax.random.uniform(streams_of[1], (NX, NY, NZ), jnp.float32) ** steps_of(streams_of[1], (NX, NY, NZ), ((0, 4), (1, 4), (2, 2)), -0.2, 0.2)), 0.01, 0.08)
    counts = draw_counts(jax.random.fold_in(streams_of[6], 71), 0)
    destination = draw_destination(jax.random.fold_in(streams_of[6], 71), 0)
    seeds = draw_seeds(jax.random.fold_in(streams_of[6], 71), 0)
    substeps = set_ends(jax.random.randint(streams_of[5], (N_WIDE, N_SEC, N_TILE, BLK_DEV, PTS), 0, MAXSUB + 1), jax.random.fold_in(streams_of[5], 1), 0, MAXSUB).astype(jnp.int32)
    return {"velocity": velocity, "viscosity": viscosity, "counts": counts, "destination": destination, "seeds": seeds, "substeps": substeps}


flow_step = 0.2
trace_step = 1.25


def neighbor(padded, dimension, offset):
    window = [slice(None), slice(1, -1), slice(1, -1), slice(1, -1)]
    length = padded.shape[dimension]
    window[dimension] = slice(1 + offset, length - 1 + offset)
    return padded[tuple(window)]


def advance(padded, viscous):
    centre = padded[:, 1:-1, 1:-1, 1:-1]
    spread = jnp.zeros_like(centre)
    laplace = jnp.zeros_like(centre)
    for component in range(3):
        dimension = component + 1
        upper_cell = neighbor(padded, dimension, 1)
        lower_cell = neighbor(padded, dimension, -1)
        flux_up = 0.25 * (centre + upper_cell) * (centre[component] + upper_cell[component])
        flux_down = 0.25 * (lower_cell + centre) * (lower_cell[component] + centre[component])
        spread = spread + (flux_up - flux_down)
        laplace = laplace + (upper_cell + lower_cell)
    laplace = laplace - 6.0 * centre
    return centre + flow_step * (viscous * laplace - spread)


def runge_kutta(offset, sampler):
    section_one = sampler(offset)
    section_two = sampler(offset + (0.5 * trace_step) * section_one)
    section_three = sampler(offset + (0.5 * trace_step) * section_two)
    section_four = sampler(offset + trace_step * section_three)
    return offset + (trace_step / 6.0) * (section_one + 2.0 * section_two + 2.0 * section_three + section_four)


def march(offset, steps_float, sampler):
    for turn_index in range(MAXSUB):
        moved_off = runge_kutta(offset, sampler)
        offset = jnp.where(turn_index < steps_float, moved_off, offset)
    return offset


def global_sampler(flattened, cells, offset):
    lowest = jnp.floor(offset)
    fraction = offset - lowest
    corner = cells + lowest.astype(jnp.int32)
    summed = jnp.zeros_like(offset)
    for step_x in range(2):
        weight_x = fraction[0] if step_x else 1.0 - fraction[0]
        cell_x = jnp.mod(corner[0] + step_x, NX)
        for step_y in range(2):
            weight_y = fraction[1] if step_y else 1.0 - fraction[1]
            cell_y = corner[1] + step_y
            inside = (cell_y >= 0) & (cell_y < NY)
            clamped = jnp.clip(cell_y, 0, NY - 1)
            for step_z in range(2):
                weight_z = fraction[2] if step_z else 1.0 - fraction[2]
                cell_z = jnp.mod(corner[2] + step_z, NZ)
                linear = (cell_x * NY + clamped) * NZ + cell_z
                values = jnp.take(flattened, linear, axis=1)
                values = jnp.where(inside, values, 0.0)
                summed = summed + (weight_x * weight_y * weight_z) * values
    return summed


def reference(velocity, viscosity, counts, destination, seeds, substeps):
    padded = jnp.pad(velocity, ((0, 0), (1, 1), (0, 0), (1, 1)), mode="wrap")
    padded = jnp.pad(padded, ((0, 0), (0, 0), (1, 1), (0, 0)))
    fresh_vel = advance(padded, viscosity)
    flattened = fresh_vel.reshape(3, -1)
    wide_ids = jnp.broadcast_to(jnp.arange(N_WIDE, dtype=jnp.int32)[:, None, None, None], destination.shape)
    sec_ids = jnp.broadcast_to(jnp.arange(N_SEC, dtype=jnp.int32)[None, :, None, None], destination.shape)
    anchor = jnp.stack([wide_ids * CX, destination * CY, sec_ids * CZ], -1)
    start_cell = (seeds + anchor[..., None]).astype(jnp.int32)
    cells = jnp.moveaxis(start_cell, 4, 0).reshape(3, -1)
    steps_float = substeps.reshape(-1)
    offset = jnp.zeros(cells.shape, jnp.float32)
    traced = march(offset, steps_float, partial(global_sampler, flattened, cells))
    traced = jnp.moveaxis(traced.reshape(3, N_WIDE, N_SEC, N_TILE, BLK_DEV, PTS), 0, 4)
    tile_ids = jnp.arange(N_TILE, dtype=jnp.int32)
    block_ids = jnp.arange(BLK_DEV, dtype=jnp.int32)
    is_live = block_ids[None, None, None, :] < counts[..., None]
    onehot = ((destination[..., None] == tile_ids) & is_live[..., None]).astype(jnp.int32)
    order_rank = jnp.sum(onehot * (jnp.cumsum(onehot, 3) - onehot), -1)
    slot_index = tile_ids[None, None, :, None] * CAP + order_rank
    target = jnp.where(is_live, destination, N_TILE)
    result = jnp.zeros((N_WIDE, N_SEC, N_TILE, SLOTS, 3, PTS), jnp.float32)
    result = result.at[wide_ids, sec_ids, target, slot_index].set(traced, mode="drop")
    return fresh_vel, result
```

```python
import functools

import jax
import jax.numpy as jnp
from jax import lax
from jax.experimental import pallas as pl
from jax.experimental.pallas import tpu as pltpu
from jax.sharding import PartitionSpec as P

CAP = 2
SUB = 8
LANE = 128

flow_step = 0.2
trace_step = 1.25

MESH = pl.DeviceIdType.MESH


def plan(sizes):
    n_wide, n_sec, n_tile = sizes
    sides = (1,) if n_sec == 2 else (1, -1)
    rows = [("row", dx, dy, 0) for dx in (-1, 0, 1) for dy in (-1, 1)]
    cols = [("col", dx, dy, dz) for dz in sides for dx in (-1, 0, 1) for dy in (-1, 0, 1)]
    planes = [("plane", dx, 0, 0) for dx in (-1, 1)] + [("visc", dx, 0, 0) for dx in (-1, 1)]
    seeds = [("seed", 0, dy, 0) for dy in range(1, n_tile)]
    return sides, cols, rows, planes, seeds


def kernel(
    sizes,
    counts_ref, dest_ref, vel_ref, visc_ref, seeds_ref, steps_ref,
    new_ref, out_ref,
    ext, shifted, dense, col_out, row_out, col_mid, col_edge, row_in, seed_out, seed_in,
    send_sem, recv_sem,
):
    n_wide, n_sec, n_tile = sizes
    _, X, Y, Z = vel_ref.shape
    YE, ZE = Y + SUB, Z + LANE
    w, s, t = lax.axis_index("wide"), lax.axis_index("sec"), lax.axis_index("tile")
    sides, cols, rows, planes, seeds = plan(sizes)
    messages = seeds + cols + rows + planes

    def device(dx, dy, dz):
        return (
            lax.rem(w + (dx + n_wide), n_wide),
            lax.rem(s + (dz + n_sec), n_sec),
            lax.rem(t + (dy + n_tile), n_tile),
        )

    peers = sorted({(dx % n_wide, dy % n_tile, dz % n_sec) for _, dx, dy, dz in messages})
    barrier = pltpu.get_barrier_semaphore()
    for peer in peers:
        pl.semaphore_signal(barrier, inc=1, device_id=device(*peer), device_id_type=MESH)

    n_blk = seeds_ref.shape[0]
    count = counts_ref[0]
    target = [jnp.where(b < count, dest_ref[b], -1) for b in range(n_blk)]
    rank = []
    for b in range(n_blk):
        r = jnp.int32(0)
        for a in range(b):
            r = r + jnp.where(target[a] == target[b], 1, 0)
        rank.append(r)
    for d in range(n_tile):
        for r in range(CAP):
            cell = jnp.zeros((3, LANE), jnp.int32)
            step = jnp.zeros((1, LANE), jnp.int32)
            for b in range(n_blk):
                hit = jnp.where((target[b] == d) & (rank[b] == r), 1, 0)
                cell = cell + seeds_ref[b] * hit
                step = step + steps_ref[b : b + 1] * hit
            seed_out[d, 4 * r : 4 * r + 3] = cell
            seed_out[d, 4 * r + 3 : 4 * r + 4] = step

    lane = lax.broadcasted_iota(jnp.int32, (Y, LANE), 1)
    packed = jnp.zeros((Y, LANE), jnp.float32)
    for c in range(4):
        for x in range(X):
            k = c * X + x
            plane = vel_ref[c, x] if c < 3 else visc_ref[x]
            if Z == LANE:
                edge = plane
            else:
                edge = jnp.where(lane < LANE // 2, plane[:, :LANE], plane[:, Z - LANE :])
            moved = pltpu.roll(edge, (4 * k + 2) % LANE, 1)
            packed = jnp.where((lane >= 4 * k) & (lane < 4 * k + 4), moved, packed)
            row_out[0, 2 * k : 2 * k + 2] = plane[0:2]
            row_out[1, 2 * k : 2 * k + 2] = plane[Y - 2 : Y]
    col_out[...] = packed

    pl.semaphore_wait(barrier, len(peers))

    copies = {}
    for m, (kind, dx, dy, dz) in enumerate(messages):
        if kind == "seed":
            src, dst = seed_out.at[lax.rem(t + dy, n_tile)], seed_in.at[t]
        elif kind == "col":
            at = (sides.index(dz), dx + 1)
            if dy == 0:
                src, dst = col_out, col_mid.at[at]
            elif dy == 1:
                src, dst = col_out.at[Y - SUB : Y], col_edge.at[at + (0,)]
            else:
                src, dst = col_out.at[0:SUB], col_edge.at[at + (1,)]
        elif kind == "row":
            src, dst = row_out.at[1 if dy == 1 else 0], row_in.at[0 if dy == 1 else 1, dx + 1]
        elif kind == "plane":
            if dx == 1:
                src, dst = vel_ref.at[:, X - 2 : X], ext.at[0:3, 0:2, 0:Y, 0:Z]
            else:
                src, dst = vel_ref.at[:, 0:2], ext.at[0:3, X + 2 : X + 4, 0:Y, 0:Z]
        else:
            if dx == 1:
                src, dst = visc_ref.at[X - 1], ext.at[3, 1, 0:Y, 0:Z]
            else:
                src, dst = visc_ref.at[0], ext.at[3, X + 2, 0:Y, 0:Z]
        copy = pltpu.make_async_remote_copy(
            src_ref=src, dst_ref=dst, send_sem=send_sem.at[m], recv_sem=recv_sem.at[m],
            device_id=device(dx, dy, dz), device_id_type=MESH,
        )
        copy.start()
        copies[kind, dx, dy, dz] = copy

    seed_in[t] = seed_out[t]
    ext[0:3, 2 : X + 2, 0:Y, 0:Z] = vel_ref[...]
    ext[3, 2 : X + 2, 0:Y, 0:Z] = visc_ref[...]

    low_open = t > 0
    high_open = t < n_tile - 1
    spans = {0: [(x, x + 2) for x in range(X)], 1: [(X - 2, 0), (X - 1, 1)], -1: [(0, X + 2), (1, X + 3)]}

    for message in rows:
        copies[message].wait_recv()
    gap = jnp.zeros((SUB - 4, Z), jnp.float32)
    for dx in (-1, 0, 1):
        for c in range(4):
            for x, here in spans[dx]:
                if c == 3 and here in (0, X + 3):
                    continue
                k = c * X + x
                high = jnp.where(high_open, row_in[1, dx + 1, 2 * k : 2 * k + 2], 0.0)
                low = jnp.where(low_open, row_in[0, dx + 1, 2 * k : 2 * k + 2], 0.0)
                ext[c, here, Y:YE, 0:Z] = jnp.concatenate([high, gap, low], 0)

    for message in cols:
        copies[message].wait_recv()
    sub8 = lax.broadcasted_iota(jnp.int32, (SUB, LANE), 0)
    keep8 = ((sub8 < SUB // 2) & high_open) | ((sub8 >= SUB // 2) & low_open)
    for dx in (-1, 0, 1):
        whole = []
        for side in range(len(sides)):
            edge = jnp.where(sub8 < SUB // 2, col_edge[side, dx + 1, 1], col_edge[side, dx + 1, 0])
            edge = jnp.where(keep8, edge, 0.0)
            whole.append(jnp.concatenate([col_mid[side, dx + 1], edge], 0))
        if len(sides) == 2:
            lane_e = lax.broadcasted_iota(jnp.int32, (YE, LANE), 1)
            whole = jnp.where(lane_e % 4 < 2, whole[0], whole[1])
        else:
            whole = whole[0]
        for c in range(4):
            for x, here in spans[dx]:
                if c == 3 and here in (0, X + 3):
                    continue
                k = c * X + x
                ext[c, here, :, Z:ZE] = pltpu.roll(whole, LANE - 4 * k - 2, 1)

    for message in planes:
        copies[message].wait_recv()

    row = lax.broadcasted_iota(jnp.int32, (YE, ZE), 0)
    keep = (row < Y) | ((row < Y + SUB // 2) & high_open) | ((row >= Y + SUB // 2) & low_open)

    def flow(i, carry):
        u = [ext[c, i + 1] for c in range(3)]
        before = [ext[c, i] for c in range(3)]
        after = [ext[c, i + 2] for c in range(3)]
        viscous = ext[3, i + 1]
        up = [[pltpu.roll(u[c], length - 1, axis) for c in range(3)] for axis, length in ((0, YE), (1, ZE))]
        for c in range(3):
            spread = (u[c] + after[c]) * (u[0] + after[0]) - (before[c] + u[c]) * (before[0] + u[0])
            laplace = after[c] + before[c]
            for axis in range(2):
                face = (u[c] + up[axis][c]) * (u[axis + 1] + up[axis][axis + 1])
                spread = spread + (face - pltpu.roll(face, 1, axis))
                laplace = laplace + (up[axis][c] + pltpu.roll(u[c], 1, axis))
            laplace = laplace - 6.0 * u[c]
            fresh = u[c] + flow_step * (viscous * laplace - 0.25 * spread)
            fresh = jnp.where(keep, fresh, 0.0)
            for dz in range(3):
                along = fresh if dz == 1 else pltpu.roll(fresh, 1 if dz == 0 else ZE - 1, 1)
                along = along[:, 0:Z]
                for dy in range(3):
                    moved = along if dy == 1 else pltpu.roll(along, 1 if dy == 0 else YE - 1, 0)
                    shifted[dy, dz, c, i] = moved[0:Y]
        return carry

    lax.fori_loop(0, X + 2, flow, 0)

    def hat(e):
        return (jnp.maximum(-e, 0.0), 1.0 - jnp.abs(e), jnp.maximum(e, 0.0))

    def trace(i, carry):
        def sample(e):
            wx, wy, wz = hat(e[0]), hat(e[1]), hat(e[2])
            result = []
            for c in range(3):
                total = None
                for dx in range(3):
                    in_x = None
                    for dy in range(3):
                        in_y = None
                        for dz in range(3):
                            term = wz[dz] * shifted[dy, dz, c, i + dx]
                            in_y = term if in_y is None else in_y + term
                        term = wy[dy] * in_y
                        in_x = term if in_x is None else in_x + term
                    term = wx[dx] * in_x
                    total = term if total is None else total + term
                result.append(total)
            return result

        k1 = [shifted[1, 1, c, i + 1] for c in range(3)]
        k2 = sample([0.5 * trace_step * k for k in k1])
        k3 = sample([0.5 * trace_step * k for k in k2])
        k4 = sample([trace_step * k for k in k3])
        for c in range(3):
            new_ref[c, i] = k1[c]
            dense[c, i] = trace_step / 6.0 * (k1[c] + 2.0 * k2[c] + 2.0 * k3[c] + k4[c])
        return carry

    lax.fori_loop(0, X, trace, 0)

    for message in seeds:
        copies[message].wait_recv()

    sub = lax.broadcasted_iota(jnp.int32, (SUB, LANE), 0)
    for d in range(n_tile):
        for r in range(CAP):
            points = [jnp.broadcast_to(seed_in[d, 4 * r + j : 4 * r + j + 1], (SUB, LANE)) for j in range(4)]
            line = points[0] * Y + points[1]
            for c in range(3):
                found = jnp.zeros((SUB, LANE), jnp.float32)
                for x in range(X):
                    for y in range(0, Y, SUB):
                        for z in range(0, Z, LANE):
                            value = jnp.take_along_axis(
                                dense[c, x, y : y + SUB, z : z + LANE], points[2] & (LANE - 1), axis=1
                            )
                            hit = (line == x * Y + y + sub) & (points[3] > 0)
                            if Z > LANE:
                                hit = hit & (points[2] >= z) & (points[2] < z + LANE)
                            found = jnp.where(hit, value, found)
                out_ref[d * CAP + r, c : c + 1] = jnp.sum(found, 0, keepdims=True)

    for message in messages:
        copies[message].wait_send()


def shards(sizes, velocity, viscosity, counts, destination, seeds, substeps):
    _, X, Y, Z = velocity.shape
    n_wide, n_sec, n_tile = sizes
    n_blk, _, n_pts = seeds.shape[3:]
    sides, cols, rows, planes, seed_msgs = plan(sizes)
    total = len(cols) + len(rows) + len(planes) + len(seed_msgs)
    vmem = pl.BlockSpec(memory_space=pltpu.VMEM)
    smem = pl.BlockSpec(memory_space=pltpu.SMEM)
    f32 = jnp.float32
    row_total = -(-8 * X // SUB) * SUB
    fresh, result = pl.pallas_call(
        functools.partial(kernel, sizes),
        out_shape=(
            jax.ShapeDtypeStruct((3, X, Y, Z), f32),
            jax.ShapeDtypeStruct((n_tile * CAP, 3, n_pts), f32),
        ),
        in_specs=[smem, smem, vmem, vmem, vmem, vmem],
        out_specs=(vmem, vmem),
        scratch_shapes=[
            pltpu.VMEM((4, X + 4, Y + SUB, Z + LANE), f32),
            pltpu.VMEM((3, 3, 3, X + 2, Y, Z), f32),
            pltpu.VMEM((3, X, Y, Z), f32),
            pltpu.VMEM((Y, LANE), f32),
            pltpu.VMEM((2, row_total, Z), f32),
            pltpu.VMEM((len(sides), 3, Y, LANE), f32),
            pltpu.VMEM((len(sides), 3, 2, SUB, LANE), f32),
            pltpu.VMEM((2, 3, row_total, Z), f32),
            pltpu.VMEM((n_tile, 4 * CAP, n_pts), jnp.int32),
            pltpu.VMEM((n_tile, 4 * CAP, n_pts), jnp.int32),
            pltpu.SemaphoreType.DMA((total,)),
            pltpu.SemaphoreType.DMA((total,)),
        ],
        compiler_params=pltpu.CompilerParams(
            collective_id=0, has_side_effects=True, vmem_limit_bytes=16 * 2**20
        ),
    )(
        counts.reshape(1), destination.reshape(n_blk), velocity, viscosity,
        seeds.reshape(n_blk, 3, n_pts), substeps.reshape(n_blk, n_pts),
    )
    return fresh, result[None, None, None]


def solution(mesh):
    sizes = tuple(mesh.shape[axis] for axis in ("wide", "sec", "tile"))
    in_specs = (
        P(None, "wide", "tile", "sec"),
        P("wide", "tile", "sec"),
        P("wide", "sec", "tile"),
        P("wide", "sec", "tile", None),
        P("wide", "sec", "tile", None, None, None),
        P("wide", "sec", "tile", None, None),
    )
    out_specs = (P(None, "wide", "tile", "sec"), P("wide", "sec", "tile", None, None, None))
    return jax.shard_map(
        functools.partial(shards, sizes), mesh=mesh, in_specs=in_specs, out_specs=out_specs, check_vma=False
    )
```

```python
import functools

import jax
import jax.numpy as jnp
from jax import lax
from jax.experimental import pallas as pl
from jax.experimental.pallas import tpu as pltpu
from jax.sharding import PartitionSpec as P

CAP = 2
SUB = 8
LANE = 128

flow_step = 0.2
trace_step = 1.25

MESH = pl.DeviceIdType.MESH


def plan(sizes):
    n_wide, n_sec, n_tile = sizes
    sides = (1,) if n_sec == 2 else (1, -1)
    rows = [("row", dx, dy, 0) for dx in (-1, 0, 1) for dy in (-1, 1)]
    cols = [("col", dx, dy, dz) for dz in sides for dx in (-1, 0, 1) for dy in (-1, 0, 1)]
    planes = [("plane", dx, 0, 0) for dx in (-1, 1)] + [("visc", dx, 0, 0) for dx in (-1, 1)]
    seeds = [("seed", 0, dy, 0) for dy in range(1, n_tile)]
    return sides, cols, rows, planes, seeds


def exchange(
    sizes,
    counts_ref, dest_hbm, vel_hbm, visc_hbm, seeds_hbm, steps_hbm,
    shifted, seed_all,
    ext, dest_ref, seeds_ref, steps_ref,
    col_out, row_out, col_mid, col_edge, row_in, seed_out, seed_in,
    send_sem, recv_sem, load_sem,
):
    n_wide, n_sec, n_tile = sizes
    _, X, Y, Z = vel_hbm.shape
    YE, ZE = Y + SUB, Z + LANE
    w, s, t = lax.axis_index("wide"), lax.axis_index("sec"), lax.axis_index("tile")
    sides, cols, rows, planes, seeds = plan(sizes)
    messages = planes + cols + rows + seeds
    low_open = t > 0
    high_open = t < n_tile - 1

    def device(dx, dy, dz):
        return (
            lax.rem(w + (dx + n_wide), n_wide),
            lax.rem(s + (dz + n_sec), n_sec),
            lax.rem(t + (dy + n_tile), n_tile),
        )

    peers = sorted({(dx % n_wide, dy % n_tile, dz % n_sec) for _, dx, dy, dz in messages})
    barrier = pltpu.get_barrier_semaphore()
    for peer in peers:
        pl.semaphore_signal(barrier, inc=1, device_id=device(*peer), device_id_type=MESH)

    own_vel = ext.at[0:3, 2 : X + 2, 0:Y, 0:Z]
    own_visc = ext.at[3, 2 : X + 2, 0:Y, 0:Z]
    loads = [
        pltpu.make_async_copy(src, dst, load_sem.at[i])
        for i, (src, dst) in enumerate((
            (vel_hbm, own_vel), (visc_hbm, own_visc), (seeds_hbm, seeds_ref),
            (steps_hbm, steps_ref), (dest_hbm, dest_ref),
        ))
    ]
    for load in loads:
        load.start()
    loads[0].wait()
    loads[1].wait()

    lane = lax.broadcasted_iota(jnp.int32, (Y, LANE), 1)
    packed = jnp.zeros((Y, LANE), jnp.float32)
    for x in range(X):
        for c in range(4):
            k = x * 4 + c
            plane = ext[c, x + 2, 0:Y, 0:Z]
            if Z == LANE:
                edge = plane
            else:
                edge = jnp.where(lane < LANE // 2, plane[:, :LANE], plane[:, Z - LANE :])
            moved = pltpu.roll(edge, (4 * k + 2) % LANE, 1)
            packed = jnp.where((lane >= 4 * k) & (lane < 4 * k + 4), moved, packed)
            row_out[0, 2 * k : 2 * k + 2] = plane[0:2]
            row_out[1, 2 * k : 2 * k + 2] = plane[Y - 2 : Y]
    col_out[...] = packed

    pl.semaphore_wait(barrier, len(peers))

    def allowed(kind, dy):
        if kind == "seed" or dy == 0:
            return None, None
        return (high_open, low_open) if dy == 1 else (low_open, high_open)

    def guarded(condition, action):
        if condition is None:
            action()
        else:
            pl.when(condition)(action)

    wide_rows = {0: (0, 8 * X), 1: (8 * X - 16, 16), -1: (0, 16)}
    copies = {}

    def send(message):
        kind, dx, dy, dz = message
        m = messages.index(message)
        if kind == "seed":
            src, dst = seed_out.at[lax.rem(t + dy, n_tile)], seed_in.at[t]
        elif kind == "col":
            at = (sides.index(dz), dx + 1)
            if dy == 0:
                src, dst = col_out, col_mid.at[at]
            elif dy == 1:
                src, dst = col_out.at[Y - SUB : Y], col_edge.at[at + (0,)]
            else:
                src, dst = col_out.at[0:SUB], col_edge.at[at + (1,)]
        elif kind == "row":
            first, size = wide_rows[dx]
            src = row_out.at[1 if dy == 1 else 0, first : first + size]
            dst = row_in.at[0 if dy == 1 else 1, dx + 1, first : first + size]
        elif kind == "plane":
            if dx == 1:
                src, dst = ext.at[0:3, X : X + 2, 0:Y, 0:Z], ext.at[0:3, 0:2, 0:Y, 0:Z]
            else:
                src, dst = ext.at[0:3, 2:4, 0:Y, 0:Z], ext.at[0:3, X + 2 : X + 4, 0:Y, 0:Z]
        else:
            if dx == 1:
                src, dst = ext.at[3, X + 1, 0:Y, 0:Z], ext.at[3, 1, 0:Y, 0:Z]
            else:
                src, dst = ext.at[3, 2, 0:Y, 0:Z], ext.at[3, X + 2, 0:Y, 0:Z]
        copy = pltpu.make_async_remote_copy(
            src_ref=src, dst_ref=dst, send_sem=send_sem.at[m], recv_sem=recv_sem.at[m],
            device_id=device(dx, dy, dz), device_id_type=MESH,
        )
        copies[message] = copy
        guarded(allowed(kind, dy)[0], copy.start)

    def arrive(group):
        for message in group:
            guarded(allowed(message[0], message[2])[1], copies[message].wait_recv)

    for message in planes + cols + rows:
        send(message)

    for load in loads[2:]:
        load.wait()
    n_blk = seeds_ref.shape[1]
    count = counts_ref[0, 0, 0]
    target = [jnp.where(b < count, dest_ref[0, 0, 0, b], -1) for b in range(n_blk)]
    rank = []
    for b in range(n_blk):
        r = jnp.int32(0)
        for a in range(b):
            r = r + jnp.where(target[a] == target[b], 1, 0)
        rank.append(r)
    for d in range(n_tile):
        for r in range(CAP):
            hits = [jnp.where((target[b] == d) & (rank[b] == r), 1, 0) for b in range(n_blk)]
            for j in range(4):
                line = jnp.zeros((1, LANE), jnp.int32)
                for b in range(n_blk):
                    source = seeds_ref[j, b : b + 1] if j < 3 else steps_ref[b : b + 1]
                    line = line + source * hits[b]
                seed_out[d, 4 * r + j : 4 * r + j + 1] = line
    for message in seeds:
        send(message)
    seed_in[t] = seed_out[t]

    spans = {0: [(x, x + 2) for x in range(X)], 1: [(X - 2, 0), (X - 1, 1)], -1: [(0, X + 2), (1, X + 3)]}

    arrive(rows)
    gap = jnp.zeros((SUB - 4, Z), jnp.float32)
    for dx in (0, -1, 1):
        for x, here in spans[dx]:
            for c in range(4):
                if c == 3 and here in (0, X + 3):
                    continue
                k = x * 4 + c
                high = jnp.where(high_open, row_in[1, dx + 1, 2 * k : 2 * k + 2], 0.0)
                low = jnp.where(low_open, row_in[0, dx + 1, 2 * k : 2 * k + 2], 0.0)
                ext[c, here, Y:YE, 0:Z] = jnp.concatenate([high, gap, low], 0)

    arrive(cols)
    sub8 = lax.broadcasted_iota(jnp.int32, (SUB, LANE), 0)
    keep8 = ((sub8 < SUB // 2) & high_open) | ((sub8 >= SUB // 2) & low_open)
    for dx in (0, -1, 1):
        whole = []
        for side in range(len(sides)):
            edge = jnp.where(sub8 < SUB // 2, col_edge[side, dx + 1, 1], col_edge[side, dx + 1, 0])
            edge = jnp.where(keep8, edge, 0.0)
            whole.append(jnp.concatenate([col_mid[side, dx + 1], edge], 0))
        if len(sides) == 2:
            lane_e = lax.broadcasted_iota(jnp.int32, (YE, LANE), 1)
            whole = jnp.where(lane_e % 4 < 2, whole[0], whole[1])
        else:
            whole = whole[0]
        for x, here in spans[dx]:
            for c in range(4):
                if c == 3 and here in (0, X + 3):
                    continue
                k = x * 4 + c
                ext[c, here, :, Z:ZE] = pltpu.roll(whole, LANE - 4 * k - 2, 1)

    arrive(planes)

    row = lax.broadcasted_iota(jnp.int32, (YE, ZE), 0)
    keep = (row < Y) | ((row < Y + SUB // 2) & high_open) | ((row >= Y + SUB // 2) & low_open)

    def flow(i, carry):
        u = [ext[c, i + 1] for c in range(3)]
        before = [ext[c, i] for c in range(3)]
        after = [ext[c, i + 2] for c in range(3)]
        viscous = ext[3, i + 1]
        up = [[pltpu.roll(u[c], length - 1, axis) for c in range(3)] for axis, length in ((0, YE), (1, ZE))]
        for c in range(3):
            spread = (u[c] + after[c]) * (u[0] + after[0]) - (before[c] + u[c]) * (before[0] + u[0])
            laplace = after[c] + before[c]
            for axis in range(2):
                face = (u[c] + up[axis][c]) * (u[axis + 1] + up[axis][axis + 1])
                spread = spread + (face - pltpu.roll(face, 1, axis))
                laplace = laplace + (up[axis][c] + pltpu.roll(u[c], 1, axis))
            laplace = laplace - 6.0 * u[c]
            fresh = u[c] + flow_step * (viscous * laplace - 0.25 * spread)
            fresh = jnp.where(keep, fresh, 0.0)
            for dz in range(3):
                along = fresh if dz == 1 else pltpu.roll(fresh, 1 if dz == 0 else ZE - 1, 1)
                along = along[:, 0:Z]
                for dy in range(3):
                    moved = along if dy == 1 else pltpu.roll(along, 1 if dy == 0 else YE - 1, 0)
                    shifted[dy, dz, c, i] = moved[0:Y]
        return carry

    lax.fori_loop(0, X + 2, flow, 0)

    arrive(seeds)
    seed_all[...] = seed_in[...]
    for message in messages:
        guarded(allowed(message[0], message[2])[0], copies[message].wait_send)


def pathlines(shifted, seed_all, new_hbm, out_hbm, dense, out_ref, new_sem, out_sem):
    _, _, _, planes, Y, Z = shifted.shape
    X = planes - 2
    writes = [
        pltpu.make_async_copy(shifted.at[1, 1, c, 1 : X + 1], new_hbm.at[c], new_sem.at[c])
        for c in range(3)
    ]
    for write in writes:
        write.start()

    def hat(e):
        return (jnp.maximum(-e, 0.0), 1.0 - jnp.abs(e), jnp.maximum(e, 0.0))

    def trace(i, carry):
        def sample(e):
            wx, wy, wz = hat(e[0]), hat(e[1]), hat(e[2])
            result = []
            for c in range(3):
                total = None
                for dx in range(3):
                    in_x = None
                    for dy in range(3):
                        in_y = None
                        for dz in range(3):
                            term = wz[dz] * shifted[dy, dz, c, i + dx]
                            in_y = term if in_y is None else in_y + term
                        term = wy[dy] * in_y
                        in_x = term if in_x is None else in_x + term
                    term = wx[dx] * in_x
                    total = term if total is None else total + term
                result.append(total)
            return result

        k1 = [shifted[1, 1, c, i + 1] for c in range(3)]
        k2 = sample([0.5 * trace_step * k for k in k1])
        k3 = sample([0.5 * trace_step * k for k in k2])
        k4 = sample([trace_step * k for k in k3])
        for c in range(3):
            dense[c, i] = trace_step / 6.0 * (k1[c] + 2.0 * k2[c] + 2.0 * k3[c] + k4[c])
        return carry

    lax.fori_loop(0, X, trace, 0)

    sub = lax.broadcasted_iota(jnp.int32, (SUB, LANE), 0)
    for d in range(seed_all.shape[0]):
        for r in range(CAP):
            points = [jnp.broadcast_to(seed_all[d, 4 * r + j : 4 * r + j + 1], (SUB, LANE)) for j in range(4)]
            line = points[0] * Y + points[1]
            for c in range(3):
                found = jnp.zeros((SUB, LANE), jnp.float32)
                for x in range(X):
                    for y in range(0, Y, SUB):
                        for z in range(0, Z, LANE):
                            value = jnp.take_along_axis(
                                dense[c, x, y : y + SUB, z : z + LANE], points[2] & (LANE - 1), axis=1
                            )
                            hit = (line == x * Y + y + sub) & (points[3] > 0)
                            if Z > LANE:
                                hit = hit & (points[2] >= z) & (points[2] < z + LANE)
                            found = jnp.where(hit, value, found)
                slot = d * CAP + r
                out_ref[c, slot : slot + 1] = jnp.sum(found, 0, keepdims=True)
    write = pltpu.make_async_copy(out_ref, out_hbm, out_sem)
    write.start()
    for other in writes:
        other.wait()
    write.wait()


def shards(sizes, velocity, viscosity, counts, destination, seeds, substeps):
    _, X, Y, Z = velocity.shape
    n_wide, n_sec, n_tile = sizes
    n_blk, _, n_pts = seeds.shape[3:]
    sides, cols, rows, planes, seed_msgs = plan(sizes)
    total = len(cols) + len(rows) + len(planes) + len(seed_msgs)
    vmem = pl.BlockSpec(memory_space=pltpu.VMEM)
    hbm = pl.BlockSpec(memory_space=pltpu.HBM)
    f32, i32 = jnp.float32, jnp.int32
    row_total = 8 * X
    shifted, seed_all = pl.pallas_call(
        functools.partial(exchange, sizes),
        out_shape=(
            jax.ShapeDtypeStruct((3, 3, 3, X + 2, Y, Z), f32),
            jax.ShapeDtypeStruct((n_tile, 4 * CAP, n_pts), i32),
        ),
        in_specs=[pl.BlockSpec(memory_space=pltpu.SMEM)] + [hbm] * 5,
        out_specs=(vmem, vmem),
        scratch_shapes=[
            pltpu.VMEM((4, X + 4, Y + SUB, Z + LANE), f32),
            pltpu.SMEM(destination.shape, i32),
            pltpu.VMEM((3, n_blk, n_pts), i32),
            pltpu.VMEM((n_blk, n_pts), i32),
            pltpu.VMEM((Y, LANE), f32),
            pltpu.VMEM((2, row_total, Z), f32),
            pltpu.VMEM((len(sides), 3, Y, LANE), f32),
            pltpu.VMEM((len(sides), 3, 2, SUB, LANE), f32),
            pltpu.VMEM((2, 3, row_total, Z), f32),
            pltpu.VMEM((n_tile, 4 * CAP, n_pts), i32),
            pltpu.VMEM((n_tile, 4 * CAP, n_pts), i32),
            pltpu.SemaphoreType.DMA((total,)),
            pltpu.SemaphoreType.DMA((total,)),
            pltpu.SemaphoreType.DMA((5,)),
        ],
        compiler_params=pltpu.CompilerParams(
            collective_id=0, has_side_effects=True, vmem_limit_bytes=16 * 2**20
        ),
    )(
        counts,
        *(pltpu.with_memory_space_constraint(value, pltpu.HBM) for value in (
            destination, velocity, viscosity,
            jnp.transpose(seeds.reshape(n_blk, 3, n_pts), (1, 0, 2)), substeps.reshape(n_blk, n_pts),
        )),
    )
    slots = n_tile * CAP
    fresh, result = pl.pallas_call(
        pathlines,
        out_shape=(
            jax.ShapeDtypeStruct((3, X, Y, Z), f32),
            jax.ShapeDtypeStruct((3, slots, n_pts), f32),
        ),
        in_specs=[vmem, vmem],
        out_specs=(hbm, hbm),
        scratch_shapes=[
            pltpu.VMEM((3, X, Y, Z), f32),
            pltpu.VMEM((3, slots, n_pts), f32),
            pltpu.SemaphoreType.DMA((3,)),
            pltpu.SemaphoreType.DMA,
        ],
        compiler_params=pltpu.CompilerParams(vmem_limit_bytes=16 * 2**20),
    )(shifted, seed_all)
    return fresh, jnp.transpose(result, (1, 0, 2))[None, None, None]


def solution(mesh):
    sizes = tuple(mesh.shape[axis] for axis in ("wide", "sec", "tile"))
    in_specs = (
        P(None, "wide", "tile", "sec"),
        P("wide", "tile", "sec"),
        P("wide", "sec", "tile"),
        P("wide", "sec", "tile", None),
        P("wide", "sec", "tile", None, None, None),
        P("wide", "sec", "tile", None, None),
    )
    out_specs = (P(None, "wide", "tile", "sec"), P("wide", "sec", "tile", None, None, None))
    return jax.shard_map(
        functools.partial(shards, sizes), mesh=mesh, in_specs=in_specs, out_specs=out_specs, check_vma=False
    )
```

```python
import functools

import jax
import jax.numpy as jnp
from jax import lax
from jax.experimental import pallas as pl
from jax.experimental.pallas import tpu as pltpu
from jax.sharding import PartitionSpec as P

CAP = 2
SUB = 8
LANE = 128

flow_step = 0.2
trace_step = 1.25

MESH = pl.DeviceIdType.MESH


def plan(sizes):
    n_wide, n_sec, n_tile = sizes
    sides = (1,) if n_sec == 2 else (1, -1)
    rows = [("row", 0, dy, 0) for dy in (-1, 1)]
    cols = [("col", 0, dy, dz) for dz in sides for dy in (-1, 1, 0)]
    planes = [("plane", dx, 0, 0) for dx in (-1, 1)] + [("visc", dx, 0, 0) for dx in (-1, 1)]
    passed = [(kind, dx, 0, 0) for kind in ("passed cols", "passed rows") for dx in (-1, 1)]
    seeds = [("seed", 0, dy, 0) for dy in range(1, n_tile)]
    return sides, cols, rows, planes, passed, seeds


def exchange(
    sizes,
    counts_ref, dest_hbm, vel_hbm, visc_hbm, seeds_hbm, steps_hbm,
    shifted, seed_all,
    ext, dest_ref, seeds_ref, steps_ref,
    col_out, row_out, col_in, row_in, seed_out, seed_in,
    send_sem, recv_sem, load_sem,
):
    n_wide, n_sec, n_tile = sizes
    _, X, Y, Z = vel_hbm.shape
    YE, ZE = Y + SUB, Z + LANE
    w, s, t = lax.axis_index("wide"), lax.axis_index("sec"), lax.axis_index("tile")
    sides, cols, rows, planes, passed, seeds = plan(sizes)
    messages = planes + cols + rows + passed + seeds
    low_open = t > 0
    high_open = t < n_tile - 1

    def device(dx, dy, dz):
        return (
            lax.rem(w + (dx + n_wide), n_wide),
            lax.rem(s + (dz + n_sec), n_sec),
            lax.rem(t + (dy + n_tile), n_tile),
        )

    peers = sorted({(dx % n_wide, dy % n_tile, dz % n_sec) for _, dx, dy, dz in messages})
    barrier = pltpu.get_barrier_semaphore()
    for peer in peers:
        pl.semaphore_signal(barrier, inc=1, device_id=device(*peer), device_id_type=MESH)

    own_vel = ext.at[0:3, 2 : X + 2, 0:Y, 0:Z]
    own_visc = ext.at[3, 2 : X + 2, 0:Y, 0:Z]
    loads = [
        pltpu.make_async_copy(src, dst, load_sem.at[i])
        for i, (src, dst) in enumerate((
            (vel_hbm, own_vel), (visc_hbm, own_visc), (seeds_hbm, seeds_ref),
            (steps_hbm, steps_ref), (dest_hbm, dest_ref),
        ))
    ]
    for load in loads:
        load.start()
    pl.semaphore_wait(barrier, len(peers))

    def allowed(kind, dy):
        if kind == "seed" or dy == 0:
            return None, None
        return (high_open, low_open) if dy == 1 else (low_open, high_open)

    def guarded(condition, action):
        if condition is None:
            action()
        else:
            pl.when(condition)(action)

    copies = {}

    def send(message):
        kind, dx, dy, dz = message
        m = messages.index(message)
        if kind == "seed":
            src, dst = seed_out.at[lax.rem(t + dy, n_tile)], seed_in.at[t]
        elif kind == "col":
            side = sides.index(dz)
            if dy == 0:
                src, dst = col_out, col_in.at[side, 1, 0:Y]
            elif dy == 1:
                src, dst = col_out.at[Y - SUB : Y], col_in.at[side, 1, Y : Y + SUB]
            else:
                src, dst = col_out.at[0:SUB], col_in.at[side, 1, Y + SUB : Y + 2 * SUB]
        elif kind == "row":
            src, dst = (row_out.at[1], row_in.at[1, :, 0]) if dy == 1 else (row_out.at[0], row_in.at[1, :, 1])
        elif kind == "passed cols":
            src, dst = col_in.at[:, 1], col_in.at[:, dx + 1]
        elif kind == "passed rows":
            first = X - 2 if dx == 1 else 0
            src, dst = row_in.at[1, first : first + 2], row_in.at[dx + 1, first : first + 2]
        elif kind == "plane":
            if dx == 1:
                src, dst = vel_hbm.at[:, X - 2 : X], ext.at[0:3, 0:2, 0:Y, 0:Z]
            else:
                src, dst = vel_hbm.at[:, 0:2], ext.at[0:3, X + 2 : X + 4, 0:Y, 0:Z]
        else:
            if dx == 1:
                src, dst = visc_hbm.at[X - 1], ext.at[3, 1, 0:Y, 0:Z]
            else:
                src, dst = visc_hbm.at[0], ext.at[3, X + 2, 0:Y, 0:Z]
        copy = pltpu.make_async_remote_copy(
            src_ref=src, dst_ref=dst, send_sem=send_sem.at[m], recv_sem=recv_sem.at[m],
            device_id=device(dx, dy, dz), device_id_type=MESH,
        )
        copies[message] = copy
        guarded(allowed(kind, dy)[0], copy.start)

    def arrive(group):
        for message in group:
            guarded(allowed(message[0], message[2])[1], copies[message].wait_recv)

    for message in planes:
        send(message)

    loads[0].wait()
    loads[1].wait()

    lane = lax.broadcasted_iota(jnp.int32, (Y, LANE), 1)
    packed = jnp.zeros((Y, LANE), jnp.float32)
    for x in range(X):
        for c in range(4):
            k = x * 4 + c
            plane = ext[c, x + 2, 0:Y, 0:Z]
            if Z == LANE:
                edge = plane
            else:
                edge = jnp.where(lane < LANE // 2, plane[:, :LANE], plane[:, Z - LANE :])
            moved = pltpu.roll(edge, (4 * k + 2) % LANE, 1)
            packed = jnp.where((lane >= 4 * k) & (lane < 4 * k + 4), moved, packed)
            row_out[0, x, 2 * c : 2 * c + 2] = plane[0:2]
            row_out[1, x, 2 * c : 2 * c + 2] = plane[Y - 2 : Y]
    col_out[...] = packed
    for message in cols + rows:
        send(message)

    for load in loads[2:]:
        load.wait()
    n_blk = seeds_ref.shape[1]
    count = counts_ref[0, 0, 0]
    target = [jnp.where(b < count, dest_ref[0, 0, 0, b], -1) for b in range(n_blk)]
    rank = []
    for b in range(n_blk):
        r = jnp.int32(0)
        for a in range(b):
            r = r + jnp.where(target[a] == target[b], 1, 0)
        rank.append(r)
    for d in range(n_tile):
        for r in range(CAP):
            hits = [jnp.where((target[b] == d) & (rank[b] == r), 1, 0) for b in range(n_blk)]
            for j in range(4):
                line = jnp.zeros((1, LANE), jnp.int32)
                for b in range(n_blk):
                    source = seeds_ref[j, b : b + 1] if j < 3 else steps_ref[b : b + 1]
                    line = line + source * hits[b]
                seed_out[d, 4 * r + j : 4 * r + j + 1] = line
    for message in seeds:
        send(message)
    seed_in[t] = seed_out[t]

    arrive(cols)
    for message in passed[0:2]:
        send(message)
    arrive(rows)
    for message in passed[2:4]:
        send(message)

    spans = {0: [(x, x + 2) for x in range(X)], 1: [(X - 2, 0), (X - 1, 1)], -1: [(0, X + 2), (1, X + 3)]}
    gap = jnp.zeros((SUB - 4, Z), jnp.float32)
    sub8 = lax.broadcasted_iota(jnp.int32, (SUB, LANE), 0)
    keep8 = ((sub8 < SUB // 2) & high_open) | ((sub8 >= SUB // 2) & low_open)
    lane_e = lax.broadcasted_iota(jnp.int32, (YE, LANE), 1)

    def unpack(dx):
        whole = []
        for side in range(len(sides)):
            low, high = (col_in[side, dx + 1, Y + n : Y + n + SUB] for n in (0, SUB))
            edge = jnp.where(keep8, jnp.where(sub8 < SUB // 2, high, low), 0.0)
            whole.append(jnp.concatenate([col_in[side, dx + 1, 0:Y], edge], 0))
        whole = whole[0] if len(sides) == 1 else jnp.where(lane_e % 4 < 2, whole[0], whole[1])
        for x, here in spans[dx]:
            for c in range(4):
                if c == 3 and here in (0, X + 3):
                    continue
                high = jnp.where(high_open, row_in[dx + 1, x, 1, 2 * c : 2 * c + 2], 0.0)
                low = jnp.where(low_open, row_in[dx + 1, x, 0, 2 * c : 2 * c + 2], 0.0)
                ext[c, here, Y:YE, 0:Z] = jnp.concatenate([high, gap, low], 0)
                ext[c, here, :, Z:ZE] = pltpu.roll(whole, LANE - 4 * (x * 4 + c) - 2, 1)

    unpack(0)

    row = lax.broadcasted_iota(jnp.int32, (YE, ZE), 0)
    keep = (row < Y) | ((row < Y + SUB // 2) & high_open) | ((row >= Y + SUB // 2) & low_open)

    def flow(i, carry):
        u = [ext[c, i + 1] for c in range(3)]
        before = [ext[c, i] for c in range(3)]
        after = [ext[c, i + 2] for c in range(3)]
        viscous = ext[3, i + 1]
        up = [[pltpu.roll(u[c], length - 1, axis) for c in range(3)] for axis, length in ((0, YE), (1, ZE))]
        for c in range(3):
            spread = (u[c] + after[c]) * (u[0] + after[0]) - (before[c] + u[c]) * (before[0] + u[0])
            laplace = after[c] + before[c]
            for axis in range(2):
                face = (u[c] + up[axis][c]) * (u[axis + 1] + up[axis][axis + 1])
                spread = spread + (face - pltpu.roll(face, 1, axis))
                laplace = laplace + (up[axis][c] + pltpu.roll(u[c], 1, axis))
            laplace = laplace - 6.0 * u[c]
            fresh = u[c] + flow_step * (viscous * laplace - 0.25 * spread)
            fresh = jnp.where(keep, fresh, 0.0)
            for dz in range(3):
                along = fresh if dz == 1 else pltpu.roll(fresh, 1 if dz == 0 else ZE - 1, 1)
                along = along[:, 0:Z]
                for dy in range(3):
                    moved = along if dy == 1 else pltpu.roll(along, 1 if dy == 0 else YE - 1, 0)
                    shifted[dy, dz, c, i] = moved[0:Y]
        return carry

    lax.fori_loop(2, X, flow, 0)
    arrive(planes + passed)
    unpack(1)
    unpack(-1)
    lax.fori_loop(0, 4, lambda n, carry: flow(n + (n // 2) * (X - 2), carry), 0)

    arrive(seeds)
    seed_all[...] = seed_in[...]
    for message in messages:
        guarded(allowed(message[0], message[2])[0], copies[message].wait_send)


def pathlines(shifted, seed_all, new_hbm, out_hbm, dense, out_ref, new_sem, out_sem):
    _, _, _, planes, Y, Z = shifted.shape
    X = planes - 2
    writes = [
        pltpu.make_async_copy(shifted.at[1, 1, c, 1 : X + 1], new_hbm.at[c], new_sem.at[c])
        for c in range(3)
    ]
    for write in writes:
        write.start()

    def hat(e):
        return (jnp.maximum(-e, 0.0), 1.0 - jnp.abs(e), jnp.maximum(e, 0.0))

    def trace(i, carry):
        def sample(e):
            wx, wy, wz = hat(e[0]), hat(e[1]), hat(e[2])
            result = []
            for c in range(3):
                total = None
                for dx in range(3):
                    in_x = None
                    for dy in range(3):
                        in_y = None
                        for dz in range(3):
                            term = wz[dz] * shifted[dy, dz, c, i + dx]
                            in_y = term if in_y is None else in_y + term
                        term = wy[dy] * in_y
                        in_x = term if in_x is None else in_x + term
                    term = wx[dx] * in_x
                    total = term if total is None else total + term
                result.append(total)
            return result

        k1 = [shifted[1, 1, c, i + 1] for c in range(3)]
        k2 = sample([0.5 * trace_step * k for k in k1])
        k3 = sample([0.5 * trace_step * k for k in k2])
        k4 = sample([trace_step * k for k in k3])
        for c in range(3):
            dense[c, i] = trace_step / 6.0 * (k1[c] + 2.0 * k2[c] + 2.0 * k3[c] + k4[c])
        return carry

    lax.fori_loop(0, X, trace, 0)

    sub = lax.broadcasted_iota(jnp.int32, (SUB, LANE), 0)
    for d in range(seed_all.shape[0]):
        for r in range(CAP):
            points = [jnp.broadcast_to(seed_all[d, 4 * r + j : 4 * r + j + 1], (SUB, LANE)) for j in range(4)]
            line = points[0] * Y + points[1]
            for c in range(3):
                found = jnp.zeros((SUB, LANE), jnp.float32)
                for x in range(X):
                    for y in range(0, Y, SUB):
                        for z in range(0, Z, LANE):
                            value = jnp.take_along_axis(
                                dense[c, x, y : y + SUB, z : z + LANE], points[2] & (LANE - 1), axis=1
                            )
                            hit = (line == x * Y + y + sub) & (points[3] > 0)
                            if Z > LANE:
                                hit = hit & (points[2] >= z) & (points[2] < z + LANE)
                            found = jnp.where(hit, value, found)
                slot = d * CAP + r
                out_ref[c, slot : slot + 1] = jnp.sum(found, 0, keepdims=True)
    write = pltpu.make_async_copy(out_ref, out_hbm, out_sem)
    write.start()
    for other in writes:
        other.wait()
    write.wait()


def shards(sizes, velocity, viscosity, counts, destination, seeds, substeps):
    _, X, Y, Z = velocity.shape
    n_wide, n_sec, n_tile = sizes
    n_blk, _, n_pts = seeds.shape[3:]
    sides, cols, rows, planes, passed, seed_msgs = plan(sizes)
    total = len(cols) + len(rows) + len(planes) + len(passed) + len(seed_msgs)
    vmem = pl.BlockSpec(memory_space=pltpu.VMEM)
    hbm = pl.BlockSpec(memory_space=pltpu.HBM)
    f32, i32 = jnp.float32, jnp.int32
    shifted, seed_all = pl.pallas_call(
        functools.partial(exchange, sizes),
        out_shape=(
            jax.ShapeDtypeStruct((3, 3, 3, X + 2, Y, Z), f32),
            jax.ShapeDtypeStruct((n_tile, 4 * CAP, n_pts), i32),
        ),
        in_specs=[pl.BlockSpec(memory_space=pltpu.SMEM)] + [hbm] * 5,
        out_specs=(vmem, vmem),
        scratch_shapes=[
            pltpu.VMEM((4, X + 4, Y + SUB, Z + LANE), f32),
            pltpu.SMEM(destination.shape, i32),
            pltpu.VMEM((3, n_blk, n_pts), i32),
            pltpu.VMEM((n_blk, n_pts), i32),
            pltpu.VMEM((Y, LANE), f32),
            pltpu.VMEM((2, X, SUB, Z), f32),
            pltpu.VMEM((len(sides), 3, Y + 2 * SUB, LANE), f32),
            pltpu.VMEM((3, X, 2, SUB, Z), f32),
            pltpu.VMEM((n_tile, 4 * CAP, n_pts), i32),
            pltpu.VMEM((n_tile, 4 * CAP, n_pts), i32),
            pltpu.SemaphoreType.DMA((total,)),
            pltpu.SemaphoreType.DMA((total,)),
            pltpu.SemaphoreType.DMA((5,)),
        ],
        compiler_params=pltpu.CompilerParams(
            collective_id=0, has_side_effects=True, vmem_limit_bytes=16 * 2**20
        ),
    )(
        counts,
        *(pltpu.with_memory_space_constraint(value, pltpu.HBM) for value in (
            destination, velocity, viscosity,
            jnp.transpose(seeds.reshape(n_blk, 3, n_pts), (1, 0, 2)), substeps.reshape(n_blk, n_pts),
        )),
    )
    slots = n_tile * CAP
    fresh, result = pl.pallas_call(
        pathlines,
        out_shape=(
            jax.ShapeDtypeStruct((3, X, Y, Z), f32),
            jax.ShapeDtypeStruct((3, slots, n_pts), f32),
        ),
        in_specs=[vmem, vmem],
        out_specs=(hbm, hbm),
        scratch_shapes=[
            pltpu.VMEM((3, X, Y, Z), f32),
            pltpu.VMEM((3, slots, n_pts), f32),
            pltpu.SemaphoreType.DMA((3,)),
            pltpu.SemaphoreType.DMA,
        ],
        compiler_params=pltpu.CompilerParams(vmem_limit_bytes=16 * 2**20),
    )(shifted, seed_all)
    return fresh, jnp.transpose(result, (1, 0, 2))[None, None, None]


def solution(mesh):
    sizes = tuple(mesh.shape[axis] for axis in ("wide", "sec", "tile"))
    in_specs = (
        P(None, "wide", "tile", "sec"),
        P("wide", "tile", "sec"),
        P("wide", "sec", "tile"),
        P("wide", "sec", "tile", None),
        P("wide", "sec", "tile", None, None, None),
        P("wide", "sec", "tile", None, None),
    )
    out_specs = (P(None, "wide", "tile", "sec"), P("wide", "sec", "tile", None, None, None))
    return jax.shard_map(
        functools.partial(shards, sizes), mesh=mesh, in_specs=in_specs, out_specs=out_specs, check_vma=False
    )
```

```python
import functools

import jax
import jax.numpy as jnp
from jax import lax
from jax.experimental import pallas as pl
from jax.experimental.pallas import tpu as pltpu
from jax.sharding import PartitionSpec as P

CAP = 2
SUB = 8
LANE = 128

flow_step = 0.2
trace_step = 1.25

MESH = pl.DeviceIdType.MESH


def plan(sizes):
    n_wide, n_sec, n_tile = sizes
    sides = (1,) if n_sec == 2 else (1, -1)
    rows = [("row", 0, dy, 0) for dy in (-1, 1)]
    cols = [("col", 0, dy, dz) for dz in sides for dy in (-1, 1, 0)]
    planes = [("plane", dx, 0, 0) for dx in (-1, 1)] + [("visc", dx, 0, 0) for dx in (-1, 1)]
    passed = [(kind, dx, 0, 0) for kind in ("passed cols", "passed rows") for dx in (-1, 1)]
    seeds = [("seed", 0, dy, 0) for dy in range(1, n_tile)]
    return sides, cols, rows, planes, passed, seeds


def exchange(
    sizes,
    counts_ref, dest_hbm, vel_hbm, visc_hbm, seeds_hbm, steps_hbm,
    shifted, seed_all,
    ext, dest_ref, seeds_ref, steps_ref,
    col_out, row_out, col_in, row_in, pass_col_out, pass_col_in, pass_row_out, pass_row_in, seed_out, seed_in,
    send_sem, recv_sem, load_sem,
):
    n_wide, n_sec, n_tile = sizes
    _, X, Y, Z = vel_hbm.shape
    YE, ZE = Y + SUB, Z + LANE
    w, s, t = lax.axis_index("wide"), lax.axis_index("sec"), lax.axis_index("tile")
    sides, cols, rows, planes, passed, seeds = plan(sizes)
    messages = planes + cols + rows + passed + seeds
    low_open = t > 0
    high_open = t < n_tile - 1

    def device(dx, dy, dz):
        return (
            lax.rem(w + (dx + n_wide), n_wide),
            lax.rem(s + (dz + n_sec), n_sec),
            lax.rem(t + (dy + n_tile), n_tile),
        )

    own_vel = ext.at[0:3, 2 : X + 2, 0:Y, 0:Z]
    own_visc = ext.at[3, 2 : X + 2, 0:Y, 0:Z]
    loads = [
        pltpu.make_async_copy(src, dst, load_sem.at[i])
        for i, (src, dst) in enumerate((
            (vel_hbm, own_vel), (visc_hbm, own_visc), (seeds_hbm, seeds_ref),
            (steps_hbm, steps_ref), (dest_hbm, dest_ref),
        ))
    ]
    for load in loads:
        load.start()

    peers = sorted({(dx % n_wide, dy % n_tile, dz % n_sec) for _, dx, dy, dz in messages})
    barrier = pltpu.get_barrier_semaphore()
    for peer in peers:
        pl.semaphore_signal(barrier, inc=1, device_id=device(*peer), device_id_type=MESH)

    pl.semaphore_wait(barrier, len(peers))

    def allowed(kind, dy):
        if kind == "seed" or dy == 0:
            return None, None
        return (high_open, low_open) if dy == 1 else (low_open, high_open)

    def guarded(condition, action):
        if condition is None:
            action()
        else:
            pl.when(condition)(action)

    copies = {}

    def send(message):
        kind, dx, dy, dz = message
        m = messages.index(message)
        if kind == "seed":
            src, dst = seed_out.at[lax.rem(t + dy, n_tile)], seed_in.at[t]
        elif kind == "col":
            side = sides.index(dz)
            if dy == 0:
                src, dst = col_out, col_in.at[side, 0:Y]
            elif dy == 1:
                src, dst = col_out.at[Y - SUB : Y], col_in.at[side, Y : Y + SUB]
            else:
                src, dst = col_out.at[0:SUB], col_in.at[side, Y + SUB : Y + 2 * SUB]
        elif kind == "row":
            src, dst = (row_out.at[1], row_in.at[:, 0]) if dy == 1 else (row_out.at[0], row_in.at[:, 1])
        elif kind == "passed cols":
            src, dst = pass_col_out.at[(dx + 1) // 2], pass_col_in.at[(dx + 1) // 2]
        elif kind == "passed rows":
            src, dst = pass_row_out.at[(dx + 1) // 2], pass_row_in.at[(dx + 1) // 2]
        elif kind == "plane":
            if dx == 1:
                src, dst = vel_hbm.at[:, X - 2 : X], ext.at[0:3, 0:2, 0:Y, 0:Z]
            else:
                src, dst = vel_hbm.at[:, 0:2], ext.at[0:3, X + 2 : X + 4, 0:Y, 0:Z]
        else:
            if dx == 1:
                src, dst = visc_hbm.at[X - 1], ext.at[3, 1, 0:Y, 0:Z]
            else:
                src, dst = visc_hbm.at[0], ext.at[3, X + 2, 0:Y, 0:Z]
        copy = pltpu.make_async_remote_copy(
            src_ref=src, dst_ref=dst, send_sem=send_sem.at[m], recv_sem=recv_sem.at[m],
            device_id=device(dx, dy, dz), device_id_type=MESH,
        )
        copies[message] = copy
        guarded(allowed(kind, dy)[0], copy.start)

    def arrive(group):
        for message in group:
            guarded(allowed(message[0], message[2])[1], copies[message].wait_recv)

    for message in planes:
        send(message)

    loads[0].wait()
    loads[1].wait()

    lane = lax.broadcasted_iota(jnp.int32, (Y, LANE), 1)
    packed = jnp.zeros((Y, LANE), jnp.float32)
    for x in range(X):
        for c in range(4):
            k = x * 4 + c
            plane = ext[c, x + 2, 0:Y, 0:Z]
            if Z == LANE:
                edge = plane
            else:
                edge = jnp.where(lane < LANE // 2, plane[:, :LANE], plane[:, Z - LANE :])
            moved = pltpu.roll(edge, (4 * k + 2) % LANE, 1)
            packed = jnp.where((lane >= 4 * k) & (lane < 4 * k + 4), moved, packed)
            row_out[0, x, 2 * c : 2 * c + 2] = plane[0:2]
            row_out[1, x, 2 * c : 2 * c + 2] = plane[Y - 2 : Y]
    col_out[...] = packed
    for message in cols + rows:
        send(message)

    for load in loads[2:]:
        load.wait()
    n_blk = seeds_ref.shape[1]
    count = counts_ref[0, 0, 0]
    target = [jnp.where(b < count, dest_ref[0, 0, 0, b], -1) for b in range(n_blk)]
    rank = []
    for b in range(n_blk):
        r = jnp.int32(0)
        for a in range(b):
            r = r + jnp.where(target[a] == target[b], 1, 0)
        rank.append(r)
    for d in range(n_tile):
        for r in range(CAP):
            hits = [jnp.where((target[b] == d) & (rank[b] == r), 1, 0) for b in range(n_blk)]
            for j in range(4):
                line = jnp.zeros((1, LANE), jnp.int32)
                for b in range(n_blk):
                    source = seeds_ref[j, b : b + 1] if j < 3 else steps_ref[b : b + 1]
                    line = line + source * hits[b]
                seed_out[d, 4 * r + j : 4 * r + j + 1] = line
    for message in seeds:
        send(message)
    seed_in[t] = seed_out[t]

    sub8 = lax.broadcasted_iota(jnp.int32, (SUB, LANE), 0)
    lane8 = lax.broadcasted_iota(jnp.int32, (SUB, LANE), 1)
    groups = Y // SUB + 2
    wide_lanes = 32
    per_tile = LANE // wide_lanes
    first_lane = {-1: 0, 1: 16 * (X - 2)}

    arrive(cols)
    for message in passed[0:2]:
        dx = message[1]
        for side in range(len(sides)):
            for tile in range(-(-groups // per_tile)):
                held = jnp.zeros((SUB, LANE), jnp.float32)
                for q in range(min(per_tile, groups - tile * per_tile)):
                    at = (tile * per_tile + q) * SUB
                    group = pltpu.roll(col_in[side, at : at + SUB], (wide_lanes * q - first_lane[dx]) % LANE, 1)
                    held = jnp.where((lane8 >= wide_lanes * q) & (lane8 < wide_lanes * (q + 1)), group, held)
                pass_col_out[(dx + 1) // 2, side, tile] = held
        send(message)
    arrive(rows)
    for message in passed[2:4]:
        dx = message[1]
        near, far = (X - 1, X - 2) if dx == 1 else (0, 1)
        n = (dx + 1) // 2
        pass_row_out[n, 0:2] = row_in[near]
        for c in range(4):
            pass_row_out[n, 2, c : c + 1] = row_in[far, 0, 2 * c + 1 : 2 * c + 2]
            pass_row_out[n, 2, 4 + c : 5 + c] = row_in[far, 1, 2 * c : 2 * c + 1]
        send(message)

    spans = {0: [(x, x + 2) for x in range(X)], 1: [(X - 2, 0), (X - 1, 1)], -1: [(0, X + 2), (1, X + 3)]}
    keep8 = ((sub8 < SUB // 2) & high_open) | ((sub8 >= SUB // 2) & low_open)
    lane_e = lax.broadcasted_iota(jnp.int32, (YE, LANE), 1)

    def unpack(dx):
        n = (dx + 1) // 2
        whole = []
        for side in range(len(sides)):
            if dx == 0:
                parts = [col_in[side, g * SUB : (g + 1) * SUB] for g in range(groups)]
            else:
                parts = [
                    pltpu.roll(
                        pass_col_in[n, side, g // per_tile],
                        (first_lane[dx] - wide_lanes * (g % per_tile)) % LANE, 1,
                    )
                    for g in range(groups)
                ]
            edge = jnp.where(keep8, jnp.where(sub8 < SUB // 2, parts[-1], parts[-2]), 0.0)
            whole.append(jnp.concatenate(parts[:-2] + [edge], 0))
        whole = whole[0] if len(sides) == 1 else jnp.where(lane_e % 4 < 2, whole[0], whole[1])
        for x, here in spans[dx]:
            far = here in (0, X + 3)
            for c in range(3 if far else 4):
                if far:
                    high, low = pass_row_in[n, 2, 4 + c : 5 + c], pass_row_in[n, 2, c : c + 1]
                elif dx == 0:
                    high, low = row_in[x, 1, 2 * c : 2 * c + 2], row_in[x, 0, 2 * c : 2 * c + 2]
                else:
                    high, low = pass_row_in[n, 1, 2 * c : 2 * c + 2], pass_row_in[n, 0, 2 * c : 2 * c + 2]
                high = jnp.where(high_open, high, 0.0)
                low = jnp.where(low_open, low, 0.0)
                gap = jnp.zeros((SUB - 2 * high.shape[0], Z), jnp.float32)
                ext[c, here, Y:YE, 0:Z] = jnp.concatenate([high, gap, low], 0)
                ext[c, here, :, Z:ZE] = pltpu.roll(whole, LANE - 4 * (x * 4 + c) - 2, 1)

    unpack(0)

    row = lax.broadcasted_iota(jnp.int32, (YE, ZE), 0)
    keep = (row < Y) | ((row < Y + SUB // 2) & high_open) | ((row >= Y + SUB // 2) & low_open)

    def flow(i, carry):
        u = [ext[c, i + 1] for c in range(3)]
        before = [ext[c, i] for c in range(3)]
        after = [ext[c, i + 2] for c in range(3)]
        viscous = ext[3, i + 1]
        up = [[pltpu.roll(u[c], length - 1, axis) for c in range(3)] for axis, length in ((0, YE), (1, ZE))]
        for c in range(3):
            spread = (u[c] + after[c]) * (u[0] + after[0]) - (before[c] + u[c]) * (before[0] + u[0])
            laplace = after[c] + before[c]
            for axis in range(2):
                face = (u[c] + up[axis][c]) * (u[axis + 1] + up[axis][axis + 1])
                spread = spread + (face - pltpu.roll(face, 1, axis))
                laplace = laplace + (up[axis][c] + pltpu.roll(u[c], 1, axis))
            laplace = laplace - 6.0 * u[c]
            fresh = u[c] + flow_step * (viscous * laplace - 0.25 * spread)
            fresh = jnp.where(keep, fresh, 0.0)
            for dz in range(3):
                along = fresh if dz == 1 else pltpu.roll(fresh, 1 if dz == 0 else ZE - 1, 1)
                along = along[:, 0:Z]
                for dy in range(3):
                    moved = along if dy == 1 else pltpu.roll(along, 1 if dy == 0 else YE - 1, 0)
                    shifted[dy, dz, c, i] = moved[0:Y]
        return carry

    lax.fori_loop(2, X, flow, 0)
    arrive(planes + passed)
    unpack(1)
    unpack(-1)
    lax.fori_loop(0, 4, lambda n, carry: flow(n + (n // 2) * (X - 2), carry), 0)

    arrive(seeds)
    seed_all[...] = seed_in[...]
    for message in messages:
        guarded(allowed(message[0], message[2])[0], copies[message].wait_send)


def pathlines(shifted, seed_all, new_hbm, out_hbm, dense, out_ref, new_sem, out_sem):
    _, _, _, planes, Y, Z = shifted.shape
    X = planes - 2
    writes = [
        pltpu.make_async_copy(shifted.at[1, 1, c, 1 : X + 1], new_hbm.at[c], new_sem.at[c])
        for c in range(3)
    ]
    for write in writes:
        write.start()

    def hat(e):
        return (jnp.maximum(-e, 0.0), 1.0 - jnp.abs(e), jnp.maximum(e, 0.0))

    def trace(i, carry):
        def sample(e):
            wx, wy, wz = hat(e[0]), hat(e[1]), hat(e[2])
            result = []
            for c in range(3):
                total = None
                for dx in range(3):
                    in_x = None
                    for dy in range(3):
                        in_y = None
                        for dz in range(3):
                            term = wz[dz] * shifted[dy, dz, c, i + dx]
                            in_y = term if in_y is None else in_y + term
                        term = wy[dy] * in_y
                        in_x = term if in_x is None else in_x + term
                    term = wx[dx] * in_x
                    total = term if total is None else total + term
                result.append(total)
            return result

        k1 = [shifted[1, 1, c, i + 1] for c in range(3)]
        k2 = sample([0.5 * trace_step * k for k in k1])
        k3 = sample([0.5 * trace_step * k for k in k2])
        k4 = sample([trace_step * k for k in k3])
        for c in range(3):
            dense[c, i] = trace_step / 6.0 * (k1[c] + 2.0 * k2[c] + 2.0 * k3[c] + k4[c])
        return carry

    lax.fori_loop(0, X, trace, 0)

    sub = lax.broadcasted_iota(jnp.int32, (SUB, LANE), 0)
    for d in range(seed_all.shape[0]):
        for r in range(CAP):
            points = [jnp.broadcast_to(seed_all[d, 4 * r + j : 4 * r + j + 1], (SUB, LANE)) for j in range(4)]
            line = points[0] * Y + points[1]
            for c in range(3):
                found = jnp.zeros((SUB, LANE), jnp.float32)
                for x in range(X):
                    for y in range(0, Y, SUB):
                        for z in range(0, Z, LANE):
                            value = jnp.take_along_axis(
                                dense[c, x, y : y + SUB, z : z + LANE], points[2] & (LANE - 1), axis=1
                            )
                            hit = (line == x * Y + y + sub) & (points[3] > 0)
                            if Z > LANE:
                                hit = hit & (points[2] >= z) & (points[2] < z + LANE)
                            found = jnp.where(hit, value, found)
                slot = d * CAP + r
                out_ref[c, slot : slot + 1] = jnp.sum(found, 0, keepdims=True)
    write = pltpu.make_async_copy(out_ref, out_hbm, out_sem)
    write.start()
    for other in writes:
        other.wait()
    write.wait()


def shards(sizes, velocity, viscosity, counts, destination, seeds, substeps):
    _, X, Y, Z = velocity.shape
    n_wide, n_sec, n_tile = sizes
    n_blk, _, n_pts = seeds.shape[3:]
    sides, cols, rows, planes, passed, seed_msgs = plan(sizes)
    total = len(cols) + len(rows) + len(planes) + len(passed) + len(seed_msgs)
    vmem = pl.BlockSpec(memory_space=pltpu.VMEM)
    hbm = pl.BlockSpec(memory_space=pltpu.HBM)
    f32, i32 = jnp.float32, jnp.int32
    shifted, seed_all = pl.pallas_call(
        functools.partial(exchange, sizes),
        out_shape=(
            jax.ShapeDtypeStruct((3, 3, 3, X + 2, Y, Z), f32),
            jax.ShapeDtypeStruct((n_tile, 4 * CAP, n_pts), i32),
        ),
        in_specs=[pl.BlockSpec(memory_space=pltpu.SMEM)] + [hbm] * 5,
        out_specs=(vmem, vmem),
        scratch_shapes=[
            pltpu.VMEM((4, X + 4, Y + SUB, Z + LANE), f32),
            pltpu.SMEM(destination.shape, i32),
            pltpu.VMEM((3, n_blk, n_pts), i32),
            pltpu.VMEM((n_blk, n_pts), i32),
            pltpu.VMEM((Y, LANE), f32),
            pltpu.VMEM((2, X, SUB, Z), f32),
            pltpu.VMEM((len(sides), Y + 2 * SUB, LANE), f32),
            pltpu.VMEM((X, 2, SUB, Z), f32),
            pltpu.VMEM((2, len(sides), -(-(Y // SUB + 2) // 4), SUB, LANE), f32),
            pltpu.VMEM((2, len(sides), -(-(Y // SUB + 2) // 4), SUB, LANE), f32),
            pltpu.VMEM((2, 3, SUB, Z), f32),
            pltpu.VMEM((2, 3, SUB, Z), f32),
            pltpu.VMEM((n_tile, 4 * CAP, n_pts), i32),
            pltpu.VMEM((n_tile, 4 * CAP, n_pts), i32),
            pltpu.SemaphoreType.DMA((total,)),
            pltpu.SemaphoreType.DMA((total,)),
            pltpu.SemaphoreType.DMA((5,)),
        ],
        compiler_params=pltpu.CompilerParams(
            collective_id=0, has_side_effects=True, vmem_limit_bytes=16 * 2**20
        ),
    )(
        counts,
        *(pltpu.with_memory_space_constraint(value, pltpu.HBM) for value in (
            destination, velocity, viscosity,
            jnp.transpose(seeds.reshape(n_blk, 3, n_pts), (1, 0, 2)), substeps.reshape(n_blk, n_pts),
        )),
    )
    slots = n_tile * CAP
    fresh, result = pl.pallas_call(
        pathlines,
        out_shape=(
            jax.ShapeDtypeStruct((3, X, Y, Z), f32),
            jax.ShapeDtypeStruct((3, slots, n_pts), f32),
        ),
        in_specs=[vmem, vmem],
        out_specs=(hbm, hbm),
        scratch_shapes=[
            pltpu.VMEM((3, X, Y, Z), f32),
            pltpu.VMEM((3, slots, n_pts), f32),
            pltpu.SemaphoreType.DMA((3,)),
            pltpu.SemaphoreType.DMA,
        ],
        compiler_params=pltpu.CompilerParams(vmem_limit_bytes=16 * 2**20),
    )(shifted, seed_all)
    return fresh, jnp.transpose(result, (1, 0, 2))[None, None, None]


def solution(mesh):
    sizes = tuple(mesh.shape[axis] for axis in ("wide", "sec", "tile"))
    in_specs = (
        P(None, "wide", "tile", "sec"),
        P("wide", "tile", "sec"),
        P("wide", "sec", "tile"),
        P("wide", "sec", "tile", None),
        P("wide", "sec", "tile", None, None, None),
        P("wide", "sec", "tile", None, None),
    )
    out_specs = (P(None, "wide", "tile", "sec"), P("wide", "sec", "tile", None, None, None))
    return jax.shard_map(
        functools.partial(shards, sizes), mesh=mesh, in_specs=in_specs, out_specs=out_specs, check_vma=False
    )
```

```python
import functools

import jax
import jax.numpy as jnp
from jax import lax
from jax.experimental import pallas as pl
from jax.experimental.pallas import tpu as pltpu
from jax.sharding import PartitionSpec as P

CAP = 2
SUB = 8
LANE = 128

flow_step = 0.2
trace_step = 1.25

MESH = pl.DeviceIdType.MESH


def plan(sizes):
    n_wide, n_sec, n_tile = sizes
    sides = (1,) if n_sec == 2 else (1, -1)
    rows = [("row", 0, dy, 0) for dy in (-1, 1)]
    cols = [("col", 0, dy, dz) for dz in sides for dy in (-1, 1, 0)]
    diagonal = [("col", dx, dy, dz) for dz in sides for dx in (-1, 1) for dy in (-1, 1, 0)]
    diagonal += [("row", dx, dy, 0) for dx in (-1, 1) for dy in (-1, 1)]
    planes = [("plane", dx, 0, 0) for dx in (-1, 1)] + [("visc", dx, 0, 0) for dx in (-1, 1)]
    seeds = [("seed", 0, dy, 0) for dy in range(1, n_tile)]
    return sides, cols, rows, planes, diagonal, seeds


def exchange(
    sizes,
    counts_ref, dest_hbm, vel_hbm, visc_hbm, seeds_hbm, steps_hbm,
    shifted, seed_all,
    ext, dest_ref, seeds_ref, steps_ref,
    mid_out, edge_out, row_out, mid_in, edge_in, row_in, seed_out, seed_in,
    send_sem, recv_sem, load_sem,
):
    n_wide, n_sec, n_tile = sizes
    _, X, Y, Z = vel_hbm.shape
    YE, ZE = Y + SUB, Z + LANE
    w, s, t = lax.axis_index("wide"), lax.axis_index("sec"), lax.axis_index("tile")
    sides, cols, rows, planes, diagonal, seeds = plan(sizes)
    messages = planes + diagonal + cols + rows + seeds
    low_open = t > 0
    high_open = t < n_tile - 1

    def device(dx, dy, dz):
        return (
            lax.rem(w + (dx + n_wide), n_wide),
            lax.rem(s + (dz + n_sec), n_sec),
            lax.rem(t + (dy + n_tile), n_tile),
        )

    own_vel = ext.at[0:3, 2 : X + 2, 0:Y, 0:Z]
    own_visc = ext.at[3, 2 : X + 2, 0:Y, 0:Z]
    loads = [
        pltpu.make_async_copy(src, dst, load_sem.at[i])
        for i, (src, dst) in enumerate((
            (vel_hbm, own_vel), (visc_hbm, own_visc), (seeds_hbm, seeds_ref),
            (steps_hbm, steps_ref), (dest_hbm, dest_ref),
        ))
    ]
    for load in loads:
        load.start()

    peers = sorted({(dx % n_wide, dy % n_tile, dz % n_sec) for _, dx, dy, dz in messages})
    barrier = pltpu.get_barrier_semaphore()
    for peer in peers:
        pl.semaphore_signal(barrier, inc=1, device_id=device(*peer), device_id_type=MESH)

    pl.semaphore_wait(barrier, len(peers))

    def allowed(kind, dy):
        if kind == "seed" or dy == 0:
            return None, None
        return (high_open, low_open) if dy == 1 else (low_open, high_open)

    def guarded(condition, action):
        if condition is None:
            action()
        else:
            pl.when(condition)(action)

    copies = {}

    def send(message):
        kind, dx, dy, dz = message
        m = messages.index(message)
        if kind == "seed":
            src, dst = seed_out.at[lax.rem(t + dy, n_tile)], seed_in.at[t]
        elif kind == "col":
            at = (sides.index(dz), dx + 1)
            if dy == 0:
                src, dst = mid_out, mid_in.at[at]
            else:
                src, dst = (edge_out.at[1], edge_in.at[at + (0,)]) if dy == 1 else (edge_out.at[0], edge_in.at[at + (1,)])
        elif kind == "row":
            span = {0: slice(0, X), 1: slice(X - 2, X), -1: slice(0, 2)}[dx]
            src = row_out.at[1 if dy == 1 else 0, span]
            dst = row_in.at[dx + 1, span, 0 if dy == 1 else 1]
        elif kind == "plane":
            if dx == 1:
                src, dst = vel_hbm.at[:, X - 2 : X], ext.at[0:3, 0:2, 0:Y, 0:Z]
            else:
                src, dst = vel_hbm.at[:, 0:2], ext.at[0:3, X + 2 : X + 4, 0:Y, 0:Z]
        else:
            if dx == 1:
                src, dst = visc_hbm.at[X - 1], ext.at[3, 1, 0:Y, 0:Z]
            else:
                src, dst = visc_hbm.at[0], ext.at[3, X + 2, 0:Y, 0:Z]
        copy = pltpu.make_async_remote_copy(
            src_ref=src, dst_ref=dst, send_sem=send_sem.at[m], recv_sem=recv_sem.at[m],
            device_id=device(dx, dy, dz), device_id_type=MESH,
        )
        copies[message] = copy
        guarded(allowed(kind, dy)[0], copy.start)

    def arrive(group):
        for message in group:
            guarded(allowed(message[0], message[2])[1], copies[message].wait_recv)

    for message in planes:
        send(message)

    loads[0].wait()
    loads[1].wait()

    lane = lax.broadcasted_iota(jnp.int32, (Y, LANE), 1)
    packed = jnp.zeros((Y, LANE), jnp.float32)
    for x in range(X):
        for c in range(4):
            k = x * 4 + c
            plane = ext[c, x + 2, 0:Y, 0:Z]
            if Z == LANE:
                edge = plane
            else:
                edge = jnp.where(lane < LANE // 2, plane[:, :LANE], plane[:, Z - LANE :])
            moved = pltpu.roll(edge, (4 * k + 2) % LANE, 1)
            packed = jnp.where((lane >= 4 * k) & (lane < 4 * k + 4), moved, packed)
            row_out[0, x, 2 * c : 2 * c + 2] = plane[0:2]
            row_out[1, x, 2 * c : 2 * c + 2] = plane[Y - 2 : Y]
    edge_out[0] = packed[0:SUB]
    edge_out[1] = packed[Y - SUB : Y]
    lane8 = lax.broadcasted_iota(jnp.int32, (SUB, LANE), 1)
    used = 16 * X
    per_tile = LANE // used
    groups = Y // SUB
    for tile in range(mid_out.shape[0]):
        held = jnp.zeros((SUB, LANE), jnp.float32)
        for q in range(min(per_tile, groups - tile * per_tile)):
            at = (tile * per_tile + q) * SUB
            group = pltpu.roll(packed[at : at + SUB], used * q, 1)
            held = jnp.where((lane8 >= used * q) & (lane8 < used * (q + 1)), group, held)
        mid_out[tile] = held
    for message in diagonal + cols + rows:
        send(message)

    for load in loads[2:]:
        load.wait()
    n_blk = seeds_ref.shape[1]
    count = counts_ref[0, 0, 0]
    target = [jnp.where(b < count, dest_ref[0, 0, 0, b], -1) for b in range(n_blk)]
    rank = []
    for b in range(n_blk):
        r = jnp.int32(0)
        for a in range(b):
            r = r + jnp.where(target[a] == target[b], 1, 0)
        rank.append(r)
    for d in range(n_tile):
        for r in range(CAP):
            hits = [jnp.where((target[b] == d) & (rank[b] == r), 1, 0) for b in range(n_blk)]
            for j in range(4):
                line = jnp.zeros((1, LANE), jnp.int32)
                for b in range(n_blk):
                    source = seeds_ref[j, b : b + 1] if j < 3 else steps_ref[b : b + 1]
                    line = line + source * hits[b]
                seed_out[d, CAP * j + r : CAP * j + r + 1] = line
    for message in seeds:
        send(message)
    seed_in[t] = seed_out[t]

    arrive(cols)
    arrive(rows)
    sub8 = lax.broadcasted_iota(jnp.int32, (SUB, LANE), 0)

    spans = {0: [(x, x + 2) for x in range(X)], 1: [(X - 2, 0), (X - 1, 1)], -1: [(0, X + 2), (1, X + 3)]}
    keep8 = ((sub8 < SUB // 2) & high_open) | ((sub8 >= SUB // 2) & low_open)
    lane_e = lax.broadcasted_iota(jnp.int32, (YE, LANE), 1)

    def unpack(dx):
        whole = []
        for side in range(len(sides)):
            edge = jnp.where(sub8 < SUB // 2, edge_in[side, dx + 1, 1], edge_in[side, dx + 1, 0])
            parts = [
                pltpu.roll(mid_in[side, dx + 1, g // per_tile], (-used * (g % per_tile)) % LANE, 1)
                for g in range(groups)
            ]
            whole.append(jnp.concatenate(parts + [jnp.where(keep8, edge, 0.0)], 0))
        whole = whole[0] if len(sides) == 1 else jnp.where(lane_e % 4 < 2, whole[0], whole[1])
        for x, here in spans[dx]:
            far = here in (0, X + 3)
            for c in range(3 if far else 4):
                high = row_in[dx + 1, x, 1, 2 * c : 2 * c + 2]
                low = row_in[dx + 1, x, 0, 2 * c : 2 * c + 2]
                high = jnp.where(high_open, high, 0.0)
                low = jnp.where(low_open, low, 0.0)
                gap = jnp.zeros((SUB - 4, Z), jnp.float32)
                ext[c, here, Y:YE, 0:Z] = jnp.concatenate([high, gap, low], 0)
                ext[c, here, :, Z:ZE] = pltpu.roll(whole, LANE - 4 * (x * 4 + c) - 2, 1)

    unpack(0)

    row = lax.broadcasted_iota(jnp.int32, (YE, ZE), 0)
    keep = (row < Y) | ((row < Y + SUB // 2) & high_open) | ((row >= Y + SUB // 2) & low_open)

    def flow(i, carry):
        u = [ext[c, i + 1] for c in range(3)]
        before = [ext[c, i] for c in range(3)]
        after = [ext[c, i + 2] for c in range(3)]
        viscous = ext[3, i + 1]
        up = [[pltpu.roll(u[c], length - 1, axis) for c in range(3)] for axis, length in ((0, YE), (1, ZE))]
        for c in range(3):
            spread = (u[c] + after[c]) * (u[0] + after[0]) - (before[c] + u[c]) * (before[0] + u[0])
            laplace = after[c] + before[c]
            for axis in range(2):
                face = (u[c] + up[axis][c]) * (u[axis + 1] + up[axis][axis + 1])
                spread = spread + (face - pltpu.roll(face, 1, axis))
                laplace = laplace + (up[axis][c] + pltpu.roll(u[c], 1, axis))
            laplace = laplace - 6.0 * u[c]
            fresh = u[c] + flow_step * (viscous * laplace - 0.25 * spread)
            fresh = jnp.where(keep, fresh, 0.0)
            for dz in range(3):
                along = fresh if dz == 1 else pltpu.roll(fresh, 1 if dz == 0 else ZE - 1, 1)
                along = along[:, 0:Z]
                for dy in range(3):
                    moved = along if dy == 1 else pltpu.roll(along, 1 if dy == 0 else YE - 1, 0)
                    shifted[dy, dz, c, i] = moved[0:Y]
        return carry

    lax.fori_loop(2, X, flow, 0)
    arrive(planes + diagonal)
    unpack(1)
    unpack(-1)
    lax.fori_loop(0, 4, lambda n, carry: flow(n + (n // 2) * (X - 2), carry), 0)

    arrive(seeds)
    for j in range(4):
        for d in range(n_tile):
            seed_all[j, CAP * d : CAP * (d + 1)] = seed_in[d, CAP * j : CAP * (j + 1)]
    for message in messages:
        guarded(allowed(message[0], message[2])[0], copies[message].wait_send)


def pathlines(shifted, seed_all, new_hbm, out_hbm, dense, out_ref, new_sem, out_sem):
    _, _, _, planes, Y, Z = shifted.shape
    X = planes - 2
    writes = [
        pltpu.make_async_copy(shifted.at[1, 1, c, 1 : X + 1], new_hbm.at[c], new_sem.at[c])
        for c in range(3)
    ]
    for write in writes:
        write.start()

    def hat(e):
        return (jnp.maximum(-e, 0.0), 1.0 - jnp.abs(e), jnp.maximum(e, 0.0))

    def trace(i, carry):
        def sample(e):
            wx, wy, wz = hat(e[0]), hat(e[1]), hat(e[2])
            result = []
            for c in range(3):
                total = None
                for dx in range(3):
                    in_x = None
                    for dy in range(3):
                        in_y = None
                        for dz in range(3):
                            term = wz[dz] * shifted[dy, dz, c, i + dx]
                            in_y = term if in_y is None else in_y + term
                        term = wy[dy] * in_y
                        in_x = term if in_x is None else in_x + term
                    term = wx[dx] * in_x
                    total = term if total is None else total + term
                result.append(total)
            return result

        k1 = [shifted[1, 1, c, i + 1] for c in range(3)]
        k2 = sample([0.5 * trace_step * k for k in k1])
        k3 = sample([0.5 * trace_step * k for k in k2])
        k4 = sample([trace_step * k for k in k3])
        for c in range(3):
            dense[c, i] = trace_step / 6.0 * (k1[c] + 2.0 * k2[c] + 2.0 * k3[c] + k4[c])
        return carry

    lax.fori_loop(0, X, trace, 0)

    slots = seed_all.shape[1]
    point_x, point_y, point_z, point_steps = (seed_all[j] for j in range(4))
    line = jnp.where(point_steps > 0, point_x * Y + point_y, -1)
    for z in range(0, Z, LANE):
        place = line if Z == LANE else jnp.where((point_z >= z) & (point_z < z + LANE), line, -1)
        index = point_z if Z == LANE else point_z & (LANE - 1)

        def look(x, found):
            found = list(found)
            for y in range(Y):
                hit = place == x * Y + y
                for c in range(3):
                    source = jnp.broadcast_to(dense[c, x, y : y + 1, z : z + LANE], (slots, LANE))
                    found[c] = jnp.where(hit, jnp.take_along_axis(source, index, axis=1), found[c])
            return tuple(found)

        start = tuple(jnp.zeros((slots, LANE), jnp.float32) if z == 0 else out_ref[c] for c in range(3))
        for c, value in enumerate(lax.fori_loop(0, X, look, start)):
            out_ref[c] = value
    write = pltpu.make_async_copy(out_ref, out_hbm, out_sem)
    write.start()
    for other in writes:
        other.wait()
    write.wait()


def shards(sizes, velocity, viscosity, counts, destination, seeds, substeps):
    _, X, Y, Z = velocity.shape
    n_wide, n_sec, n_tile = sizes
    n_blk, _, n_pts = seeds.shape[3:]
    sides, cols, rows, planes, diagonal, seed_msgs = plan(sizes)
    total = len(cols) + len(rows) + len(planes) + len(diagonal) + len(seed_msgs)
    vmem = pl.BlockSpec(memory_space=pltpu.VMEM)
    hbm = pl.BlockSpec(memory_space=pltpu.HBM)
    f32, i32 = jnp.float32, jnp.int32
    mid_tiles = -(-(Y // SUB) // (LANE // (16 * X)))
    shifted, seed_all = pl.pallas_call(
        functools.partial(exchange, sizes),
        out_shape=(
            jax.ShapeDtypeStruct((3, 3, 3, X + 2, Y, Z), f32),
            jax.ShapeDtypeStruct((4, n_tile * CAP, n_pts), i32),
        ),
        in_specs=[pl.BlockSpec(memory_space=pltpu.SMEM)] + [hbm] * 5,
        out_specs=(vmem, vmem),
        scratch_shapes=[
            pltpu.VMEM((4, X + 4, Y + SUB, Z + LANE), f32),
            pltpu.SMEM(destination.shape, i32),
            pltpu.VMEM((3, n_blk, n_pts), i32),
            pltpu.VMEM((n_blk, n_pts), i32),
            pltpu.VMEM((mid_tiles, SUB, LANE), f32),
            pltpu.VMEM((2, SUB, LANE), f32),
            pltpu.VMEM((2, X, SUB, Z), f32),
            pltpu.VMEM((len(sides), 3, mid_tiles, SUB, LANE), f32),
            pltpu.VMEM((len(sides), 3, 2, SUB, LANE), f32),
            pltpu.VMEM((3, X, 2, SUB, Z), f32),
            pltpu.VMEM((n_tile, 4 * CAP, n_pts), i32),
            pltpu.VMEM((n_tile, 4 * CAP, n_pts), i32),
            pltpu.SemaphoreType.DMA((total,)),
            pltpu.SemaphoreType.DMA((total,)),
            pltpu.SemaphoreType.DMA((5,)),
        ],
        compiler_params=pltpu.CompilerParams(
            collective_id=0, has_side_effects=True, vmem_limit_bytes=16 * 2**20
        ),
    )(
        counts,
        *(pltpu.with_memory_space_constraint(value, pltpu.HBM) for value in (
            destination, velocity, viscosity,
            jnp.transpose(seeds.reshape(n_blk, 3, n_pts), (1, 0, 2)), substeps.reshape(n_blk, n_pts),
        )),
    )
    slots = n_tile * CAP
    fresh, result = pl.pallas_call(
        pathlines,
        out_shape=(
            jax.ShapeDtypeStruct((3, X, Y, Z), f32),
            jax.ShapeDtypeStruct((3, slots, n_pts), f32),
        ),
        in_specs=[vmem, vmem],
        out_specs=(hbm, hbm),
        scratch_shapes=[
            pltpu.VMEM((3, X, Y, Z), f32),
            pltpu.VMEM((3, slots, n_pts), f32),
            pltpu.SemaphoreType.DMA((3,)),
            pltpu.SemaphoreType.DMA,
        ],
        compiler_params=pltpu.CompilerParams(vmem_limit_bytes=16 * 2**20),
    )(shifted, seed_all)
    return fresh, jnp.transpose(result, (1, 0, 2))[None, None, None]


def solution(mesh):
    sizes = tuple(mesh.shape[axis] for axis in ("wide", "sec", "tile"))
    in_specs = (
        P(None, "wide", "tile", "sec"),
        P("wide", "tile", "sec"),
        P("wide", "sec", "tile"),
        P("wide", "sec", "tile", None),
        P("wide", "sec", "tile", None, None, None),
        P("wide", "sec", "tile", None, None),
    )
    out_specs = (P(None, "wide", "tile", "sec"), P("wide", "sec", "tile", None, None, None))
    return jax.shard_map(
        functools.partial(shards, sizes), mesh=mesh, in_specs=in_specs, out_specs=out_specs, check_vma=False
    )
```

```python
import functools

import jax
import jax.numpy as jnp
from jax import lax
from jax.experimental import pallas as pl
from jax.experimental.pallas import tpu as pltpu
from jax.sharding import PartitionSpec as P

CAP = 2
SUB = 8
LANE = 128

flow_step = 0.2
trace_step = 1.25

MESH = pl.DeviceIdType.MESH


def plan(sizes):
    n_wide, n_sec, n_tile = sizes
    sides = (1,) if n_sec == 2 else (1, -1)
    rows = [("row", 0, dy, 0) for dy in (-1, 1)]
    cols = [("col", 0, dy, dz) for dz in sides for dy in (-1, 1, 0)]
    planes = [("plane", dx, 0, 0) for dx in (-1, 1)]
    passed = [("passed", dx, 0, 0) for dx in (-1, 1)]
    seeds = [("seed", 0, dy, 0) for dy in range(1, n_tile)]
    return sides, cols, rows, planes, passed, seeds


def exchange(
    sizes,
    counts_ref, dest_hbm, vel_hbm, visc_hbm, seeds_hbm, steps_hbm,
    shifted, seed_all,
    ext, dest_ref, seeds_ref, steps_ref,
    col_out, row_out, col_in, row_in, pass_out, pass_in, seed_out, seed_in,
    send_sem, recv_sem, load_sem,
):
    n_wide, n_sec, n_tile = sizes
    _, X, Y, Z = vel_hbm.shape
    YE, ZE = Y + SUB, Z + LANE
    w, s, t = lax.axis_index("wide"), lax.axis_index("sec"), lax.axis_index("tile")
    sides, cols, rows, planes, passed, seeds = plan(sizes)
    messages = planes + cols + rows + passed + seeds
    low_open = t > 0
    high_open = t < n_tile - 1

    def shift(position, step, size):
        if step % size == 0:
            return position
        moved = position + step % size
        return jnp.where(moved >= size, moved - size, moved)

    w_of = [shift(w, step, n_wide) for step in (0, 1, -1)]
    s_of = [shift(s, step, n_sec) for step in (0, 1, -1)]
    t_of = [shift(t, step, n_tile) for step in range(n_tile)]

    def device(dx, dy, dz):
        return (w_of[dx], s_of[dz], t_of[dy])

    own_vel = ext.at[0:3, 2 : X + 2, 0:Y, 0:Z]
    own_visc = ext.at[3, 2 : X + 2, 0:Y, 0:Z]
    loads = [
        pltpu.make_async_copy(src, dst, load_sem.at[i])
        for i, (src, dst) in enumerate((
            (vel_hbm, own_vel), (visc_hbm, own_visc), (seeds_hbm, seeds_ref),
            (steps_hbm, steps_ref), (dest_hbm, dest_ref),
        ))
    ]
    for load in loads:
        load.start()

    peers = {}
    for _, dx, dy, dz in messages:
        peers.setdefault((dx % n_wide, dy % n_tile, dz % n_sec), (dx, dy, dz))
    barrier = pltpu.get_barrier_semaphore()
    for peer in peers.values():
        pl.semaphore_signal(barrier, inc=1, device_id=device(*peer), device_id_type=MESH)

    pl.semaphore_wait(barrier, len(peers))

    def allowed(kind, dy):
        if kind == "seed" or dy == 0:
            return None, None
        return (high_open, low_open) if dy == 1 else (low_open, high_open)

    def guarded(condition, action):
        if condition is None:
            action()
        else:
            pl.when(condition)(action)

    copies = {}

    def send(message):
        kind, dx, dy, dz = message
        m = messages.index(message)
        if kind == "seed":
            src, dst = seed_out.at[t_of[dy]], seed_in.at[t]
        elif kind == "col":
            side = sides.index(dz)
            if dy == 0:
                src, dst = col_out, col_in.at[side, 0:Y]
            elif dy == 1:
                src, dst = col_out.at[Y - SUB : Y], col_in.at[side, Y : Y + SUB]
            else:
                src, dst = col_out.at[0:SUB], col_in.at[side, Y + SUB : Y + 2 * SUB]
        elif kind == "row":
            src, dst = (row_out.at[1], row_in.at[:, 0]) if dy == 1 else (row_out.at[0], row_in.at[:, 1])
        elif kind == "passed":
            src, dst = pass_out.at[(dx + 1) // 2], pass_in.at[(dx + 1) // 2]
        elif dx == 1:
            src, dst = vel_hbm.at[:, X - 2 : X], ext.at[0:3, 0:2, 0:Y, 0:Z]
        else:
            src, dst = vel_hbm.at[:, 0:2], ext.at[0:3, X + 2 : X + 4, 0:Y, 0:Z]
        copy = pltpu.make_async_remote_copy(
            src_ref=src, dst_ref=dst, send_sem=send_sem.at[m], recv_sem=recv_sem.at[m],
            device_id=device(dx, dy, dz), device_id_type=MESH,
        )
        copies[message] = copy
        guarded(allowed(kind, dy)[0], copy.start)

    def arrive(group):
        for message in group:
            guarded(allowed(message[0], message[2])[1], copies[message].wait_recv)

    for message in planes:
        send(message)

    loads[0].wait()
    loads[1].wait()

    lane = lax.broadcasted_iota(jnp.int32, (Y, LANE), 1)
    packed = jnp.zeros((Y, LANE), jnp.float32)
    for x in range(X):
        for c in range(4):
            k = x * 4 + c
            plane = ext[c, x + 2, 0:Y, 0:Z]
            if Z == LANE:
                edge = plane
            else:
                edge = jnp.where(lane < LANE // 2, plane[:, :LANE], plane[:, Z - LANE :])
            moved = pltpu.roll(edge, (4 * k + 2) % LANE, 1)
            packed = jnp.where((lane >= 4 * k) & (lane < 4 * k + 4), moved, packed)
            row_out[0, x, 2 * c : 2 * c + 2] = plane[0:2]
            row_out[1, x, 2 * c : 2 * c + 2] = plane[Y - 2 : Y]
    col_out[...] = packed
    for message in cols + rows:
        send(message)

    for load in loads[2:]:
        load.wait()
    n_blk = seeds_ref.shape[1]
    count = counts_ref[0, 0, 0]
    target = [jnp.where(b < count, dest_ref[0, 0, 0, b], -1) for b in range(n_blk)]
    rank = []
    for b in range(n_blk):
        r = jnp.int32(0)
        for a in range(b):
            r = r + jnp.where(target[a] == target[b], 1, 0)
        rank.append(r)
    for d in range(n_tile):
        for r in range(CAP):
            hits = [jnp.where((target[b] == d) & (rank[b] == r), 1, 0) for b in range(n_blk)]
            for j in range(4):
                line = jnp.zeros((1, LANE), jnp.int32)
                for b in range(n_blk):
                    source = seeds_ref[j, b : b + 1] if j < 3 else steps_ref[b : b + 1]
                    line = line + source * hits[b]
                seed_out[d, 4 * r + j : 4 * r + j + 1] = line
    for message in seeds:
        send(message)
    seed_in[t] = seed_out[t]

    sub8 = lax.broadcasted_iota(jnp.int32, (SUB, LANE), 0)
    lane8 = lax.broadcasted_iota(jnp.int32, (SUB, LANE), 1)
    groups = Y // SUB + 2
    wide_lanes = 32
    per_tile = LANE // wide_lanes
    first_lane = {-1: 0, 1: 16 * (X - 2)}
    near_of = {-1: 0, 1: X - 1}
    far_of = {-1: 1, 1: X - 2}
    lanes_of = [slice(z, z + LANE) for z in range(0, Z, LANE)]
    parts_z = len(lanes_of)
    visc_at = 3 * parts_z
    cols_at = visc_at + parts_z * (Y // SUB)
    col_tiles = -(-groups // per_tile)

    for message in passed:
        dx = message[1]
        n = (dx + 1) // 2
        for z, lanes in enumerate(lanes_of):
            for y in range(Y // SUB):
                pass_out[n, visc_at + z * (Y // SUB) + y] = ext[3, near_of[dx] + 2, y * SUB : (y + 1) * SUB, lanes]
    arrive(cols)
    for message in passed:
        dx = message[1]
        for side in range(len(sides)):
            for tile in range(col_tiles):
                held = jnp.zeros((SUB, LANE), jnp.float32)
                for q in range(min(per_tile, groups - tile * per_tile)):
                    at = (tile * per_tile + q) * SUB
                    group = pltpu.roll(col_in[side, at : at + SUB], (wide_lanes * q - first_lane[dx]) % LANE, 1)
                    held = jnp.where((lane8 >= wide_lanes * q) & (lane8 < wide_lanes * (q + 1)), group, held)
                pass_out[(dx + 1) // 2, cols_at + side * col_tiles + tile] = held
    arrive(rows)
    for message in passed:
        dx = message[1]
        n = (dx + 1) // 2
        near, far = near_of[dx], far_of[dx]
        for z, lanes in enumerate(lanes_of):
            pass_out[n, 3 * z] = row_in[near, 0, :, lanes]
            pass_out[n, 3 * z + 1] = row_in[near, 1, :, lanes]
            for c in range(4):
                pass_out[n, 3 * z + 2, c : c + 1] = row_in[far, 0, 2 * c + 1 : 2 * c + 2, lanes]
                pass_out[n, 3 * z + 2, 4 + c : 5 + c] = row_in[far, 1, 2 * c : 2 * c + 1, lanes]
        send(message)

    spans = {0: [(x, x + 2) for x in range(X)], 1: [(X - 2, 0), (X - 1, 1)], -1: [(0, X + 2), (1, X + 3)]}
    keep8 = ((sub8 < SUB // 2) & high_open) | ((sub8 >= SUB // 2) & low_open)
    lane_e = lax.broadcasted_iota(jnp.int32, (YE, LANE), 1)

    def unpack(dx):
        n = (dx + 1) // 2
        whole = []
        for side in range(len(sides)):
            if dx == 0:
                parts = [col_in[side, g * SUB : (g + 1) * SUB] for g in range(groups)]
            else:
                parts = [
                    pltpu.roll(
                        pass_in[n, cols_at + side * col_tiles + g // per_tile],
                        (first_lane[dx] - wide_lanes * (g % per_tile)) % LANE, 1,
                    )
                    for g in range(groups)
                ]
            edge = jnp.where(keep8, jnp.where(sub8 < SUB // 2, parts[-1], parts[-2]), 0.0)
            whole.append(jnp.concatenate(parts[:-2] + [edge], 0))
        whole = whole[0] if len(sides) == 1 else jnp.where(lane_e % 4 < 2, whole[0], whole[1])
        for x, here in spans[dx]:
            far = here in (0, X + 3)
            for c in range(3 if far else 4):
                for z, lanes in enumerate(lanes_of):
                    if far:
                        high, low = pass_in[n, 3 * z + 2, 4 + c : 5 + c], pass_in[n, 3 * z + 2, c : c + 1]
                    elif dx == 0:
                        high, low = (row_in[x, side, 2 * c : 2 * c + 2, lanes] for side in (1, 0))
                    else:
                        high, low = (pass_in[n, 3 * z + side, 2 * c : 2 * c + 2] for side in (1, 0))
                    high = jnp.where(high_open, high, 0.0)
                    low = jnp.where(low_open, low, 0.0)
                    gap = jnp.zeros((SUB - 2 * high.shape[0], LANE), jnp.float32)
                    ext[c, here, Y:YE, lanes] = jnp.concatenate([high, gap, low], 0)
                    if c == 3 and dx != 0:
                        for y in range(Y // SUB):
                            ext[c, here, y * SUB : (y + 1) * SUB, lanes] = pass_in[n, visc_at + z * (Y // SUB) + y]
                ext[c, here, :, Z:ZE] = pltpu.roll(whole, LANE - 4 * (x * 4 + c) - 2, 1)

    unpack(0)

    row = lax.broadcasted_iota(jnp.int32, (YE, ZE), 0)
    keep = (row < Y) | ((row < Y + SUB // 2) & high_open) | ((row >= Y + SUB // 2) & low_open)

    def flow(i, carry):
        u = [ext[c, i + 1] for c in range(3)]
        before = [ext[c, i] for c in range(3)]
        after = [ext[c, i + 2] for c in range(3)]
        viscous = ext[3, i + 1]
        up = [[pltpu.roll(u[c], length - 1, axis) for c in range(3)] for axis, length in ((0, YE), (1, ZE))]
        for c in range(3):
            spread = (u[c] + after[c]) * (u[0] + after[0]) - (before[c] + u[c]) * (before[0] + u[0])
            laplace = after[c] + before[c]
            for axis in range(2):
                face = (u[c] + up[axis][c]) * (u[axis + 1] + up[axis][axis + 1])
                spread = spread + (face - pltpu.roll(face, 1, axis))
                laplace = laplace + (up[axis][c] + pltpu.roll(u[c], 1, axis))
            laplace = laplace - 6.0 * u[c]
            fresh = u[c] + flow_step * (viscous * laplace - 0.25 * spread)
            fresh = jnp.where(keep, fresh, 0.0)
            for dz in range(3):
                along = fresh if dz == 1 else pltpu.roll(fresh, 1 if dz == 0 else ZE - 1, 1)
                along = along[:, 0:Z]
                for dy in range(3):
                    moved = along if dy == 1 else pltpu.roll(along, 1 if dy == 0 else YE - 1, 0)
                    shifted[dy, dz, c, i] = moved[0:Y]
        return carry

    lax.fori_loop(2, X, flow, 0)
    arrive(planes + passed)
    unpack(1)
    unpack(-1)
    lax.fori_loop(0, 4, lambda n, carry: flow(jnp.where(n < 2, n, n + (X - 2)), carry), 0)

    arrive(seeds)
    seed_all[...] = seed_in[...]
    for message in messages:
        guarded(allowed(message[0], message[2])[0], copies[message].wait_send)


def pathlines(shifted, seed_all, new_hbm, out_hbm, dense, out_ref, new_sem, out_sem):
    _, _, _, planes, Y, Z = shifted.shape
    X = planes - 2
    writes = [
        pltpu.make_async_copy(shifted.at[1, 1, c, 1 : X + 1], new_hbm.at[c], new_sem.at[c])
        for c in range(3)
    ]
    for write in writes:
        write.start()

    def hat(e):
        return (jnp.maximum(-e, 0.0), 1.0 - jnp.abs(e), jnp.maximum(e, 0.0))

    def trace(i, carry):
        def sample(e):
            wx, wy, wz = hat(e[0]), hat(e[1]), hat(e[2])
            result = []
            for c in range(3):
                total = None
                for dx in range(3):
                    in_x = None
                    for dy in range(3):
                        in_y = None
                        for dz in range(3):
                            term = wz[dz] * shifted[dy, dz, c, i + dx]
                            in_y = term if in_y is None else in_y + term
                        term = wy[dy] * in_y
                        in_x = term if in_x is None else in_x + term
                    term = wx[dx] * in_x
                    total = term if total is None else total + term
                result.append(total)
            return result

        k1 = [shifted[1, 1, c, i + 1] for c in range(3)]
        k2 = sample([0.5 * trace_step * k for k in k1])
        k3 = sample([0.5 * trace_step * k for k in k2])
        k4 = sample([trace_step * k for k in k3])
        for c in range(3):
            dense[c, i] = trace_step / 6.0 * (k1[c] + 2.0 * k2[c] + 2.0 * k3[c] + k4[c])
        return carry

    lax.fori_loop(0, X, trace, 0)

    sub = lax.broadcasted_iota(jnp.int32, (SUB, LANE), 0)
    for d in range(seed_all.shape[0]):
        for r in range(CAP):
            points = [jnp.broadcast_to(seed_all[d, 4 * r + j : 4 * r + j + 1], (SUB, LANE)) for j in range(4)]
            line = points[0] * Y + points[1]
            for c in range(3):
                found = jnp.zeros((SUB, LANE), jnp.float32)
                for x in range(X):
                    for y in range(0, Y, SUB):
                        for z in range(0, Z, LANE):
                            value = jnp.take_along_axis(
                                dense[c, x, y : y + SUB, z : z + LANE], points[2] & (LANE - 1), axis=1
                            )
                            hit = (line == x * Y + y + sub) & (points[3] > 0)
                            if Z > LANE:
                                hit = hit & (points[2] >= z) & (points[2] < z + LANE)
                            found = jnp.where(hit, value, found)
                slot = d * CAP + r
                out_ref[c, slot : slot + 1] = jnp.sum(found, 0, keepdims=True)
    write = pltpu.make_async_copy(out_ref, out_hbm, out_sem)
    write.start()
    for other in writes:
        other.wait()
    write.wait()


def shards(sizes, velocity, viscosity, counts, destination, seeds, substeps):
    _, X, Y, Z = velocity.shape
    n_wide, n_sec, n_tile = sizes
    n_blk, _, n_pts = seeds.shape[3:]
    sides, cols, rows, planes, passed, seed_msgs = plan(sizes)
    total = len(cols) + len(rows) + len(planes) + len(passed) + len(seed_msgs)
    vmem = pl.BlockSpec(memory_space=pltpu.VMEM)
    hbm = pl.BlockSpec(memory_space=pltpu.HBM)
    f32, i32 = jnp.float32, jnp.int32
    pass_tiles = (Z // LANE) * (3 + Y // SUB) + len(sides) * -(-(Y // SUB + 2) // 4)
    shifted, seed_all = pl.pallas_call(
        functools.partial(exchange, sizes),
        out_shape=(
            jax.ShapeDtypeStruct((3, 3, 3, X + 2, Y, Z), f32),
            jax.ShapeDtypeStruct((n_tile, 4 * CAP, n_pts), i32),
        ),
        in_specs=[pl.BlockSpec(memory_space=pltpu.SMEM)] + [hbm] * 5,
        out_specs=(vmem, vmem),
        scratch_shapes=[
            pltpu.VMEM((4, X + 4, Y + SUB, Z + LANE), f32),
            pltpu.SMEM(destination.shape, i32),
            pltpu.VMEM((3, n_blk, n_pts), i32),
            pltpu.VMEM((n_blk, n_pts), i32),
            pltpu.VMEM((Y, LANE), f32),
            pltpu.VMEM((2, X, SUB, Z), f32),
            pltpu.VMEM((len(sides), Y + 2 * SUB, LANE), f32),
            pltpu.VMEM((X, 2, SUB, Z), f32),
            pltpu.VMEM((2, pass_tiles, SUB, LANE), f32),
            pltpu.VMEM((2, pass_tiles, SUB, LANE), f32),
            pltpu.VMEM((n_tile, 4 * CAP, n_pts), i32),
            pltpu.VMEM((n_tile, 4 * CAP, n_pts), i32),
            pltpu.SemaphoreType.DMA((total,)),
            pltpu.SemaphoreType.DMA((total,)),
            pltpu.SemaphoreType.DMA((5,)),
        ],
        compiler_params=pltpu.CompilerParams(
            collective_id=0, has_side_effects=True, vmem_limit_bytes=16 * 2**20
        ),
    )(
        counts,
        *(pltpu.with_memory_space_constraint(value, pltpu.HBM) for value in (
            destination, velocity, viscosity,
            jnp.transpose(seeds.reshape(n_blk, 3, n_pts), (1, 0, 2)), substeps.reshape(n_blk, n_pts),
        )),
    )
    slots = n_tile * CAP
    fresh, result = pl.pallas_call(
        pathlines,
        out_shape=(
            jax.ShapeDtypeStruct((3, X, Y, Z), f32),
            jax.ShapeDtypeStruct((3, slots, n_pts), f32),
        ),
        in_specs=[vmem, vmem],
        out_specs=(hbm, hbm),
        scratch_shapes=[
            pltpu.VMEM((3, X, Y, Z), f32),
            pltpu.VMEM((3, slots, n_pts), f32),
            pltpu.SemaphoreType.DMA((3,)),
            pltpu.SemaphoreType.DMA,
        ],
        compiler_params=pltpu.CompilerParams(vmem_limit_bytes=16 * 2**20),
    )(shifted, seed_all)
    return fresh, jnp.transpose(result, (1, 0, 2))[None, None, None]


def solution(mesh):
    sizes = tuple(mesh.shape[axis] for axis in ("wide", "sec", "tile"))
    in_specs = (
        P(None, "wide", "tile", "sec"),
        P("wide", "tile", "sec"),
        P("wide", "sec", "tile"),
        P("wide", "sec", "tile", None),
        P("wide", "sec", "tile", None, None, None),
        P("wide", "sec", "tile", None, None),
    )
    out_specs = (P(None, "wide", "tile", "sec"), P("wide", "sec", "tile", None, None, None))
    return jax.shard_map(
        functools.partial(shards, sizes), mesh=mesh, in_specs=in_specs, out_specs=out_specs, check_vma=False
    )
```

```python
import functools

import jax
import jax.numpy as jnp
from jax import lax
from jax.experimental import pallas as pl
from jax.experimental.pallas import tpu as pltpu
from jax.sharding import PartitionSpec as P

CAP = 2
SUB = 8
LANE = 128

flow_step = 0.2
trace_step = 1.25

MESH = pl.DeviceIdType.MESH


def plan(sizes):
    n_wide, n_sec, n_tile = sizes
    sides = (1,) if n_sec == 2 else (1, -1)
    rows = [("row", 0, dy, 0) for dy in (-1, 1)]
    cols = [("col", 0, dy, dz) for dz in sides for dy in (-1, 1, 0)]
    planes = [("plane", dx, 0, 0) for dx in (-1, 1)]
    passed = [("passed", dx, 0, 0) for dx in (-1, 1)]
    seeds = [("seed", 0, dy, 0) for dy in range(1, n_tile)]
    return sides, cols, rows, planes, passed, seeds


def exchange(
    sizes,
    counts_ref, dest_hbm, vel_hbm, visc_hbm, seeds_hbm, steps_hbm,
    shifted, seed_all,
    ext, dest_ref, seeds_ref, steps_ref,
    col_out, row_out, col_in, row_in, pass_out, pass_in, seed_out, seed_in,
    send_sem, recv_sem, load_sem,
):
    n_wide, n_sec, n_tile = sizes
    _, X, Y, Z = vel_hbm.shape
    YE, ZE = Y + SUB, Z + LANE
    w, s, t = lax.axis_index("wide"), lax.axis_index("sec"), lax.axis_index("tile")
    sides, cols, rows, planes, passed, seeds = plan(sizes)
    messages = planes + cols + rows + passed + seeds
    low_open = t > 0
    high_open = t < n_tile - 1

    def shift(position, step, size):
        if step % size == 0:
            return position
        moved = position + step % size
        return jnp.where(moved >= size, moved - size, moved)

    w_of = [shift(w, step, n_wide) for step in (0, 1, -1)]
    s_of = [shift(s, step, n_sec) for step in (0, 1, -1)]
    t_of = [shift(t, step, n_tile) for step in range(n_tile)]

    def device(dx, dy, dz):
        return (w_of[dx], s_of[dz], t_of[dy])

    own_vel = ext.at[0:3, 2 : X + 2, 0:Y, 0:Z]
    own_visc = ext.at[3, 2 : X + 2, 0:Y, 0:Z]
    loads = [
        pltpu.make_async_copy(src, dst, load_sem.at[i])
        for i, (src, dst) in enumerate((
            (vel_hbm, own_vel), (visc_hbm, own_visc), (seeds_hbm, seeds_ref),
            (steps_hbm, steps_ref), (dest_hbm, dest_ref),
        ))
    ]
    for load in loads:
        load.start()

    peers = {}
    for _, dx, dy, dz in messages:
        peers.setdefault((dx % n_wide, dy % n_tile, dz % n_sec), (dx, dy, dz))
    barrier = pltpu.get_barrier_semaphore()
    for peer in peers.values():
        pl.semaphore_signal(barrier, inc=1, device_id=device(*peer), device_id_type=MESH)

    pl.semaphore_wait(barrier, len(peers))

    def allowed(kind, dy):
        if kind == "seed" or dy == 0:
            return None, None
        return (high_open, low_open) if dy == 1 else (low_open, high_open)

    def guarded(condition, action):
        if condition is None:
            action()
        else:
            pl.when(condition)(action)

    copies = {}

    def prepare(message):
        kind, dx, dy, dz = message
        m = messages.index(message)
        if kind == "seed":
            src, dst = seed_out.at[t_of[dy]], seed_in.at[t]
        elif kind == "col":
            side = sides.index(dz)
            if dy == 0:
                src, dst = col_out, col_in.at[side, 0:Y]
            elif dy == 1:
                src, dst = col_out.at[Y - SUB : Y], col_in.at[side, Y : Y + SUB]
            else:
                src, dst = col_out.at[0:SUB], col_in.at[side, Y + SUB : Y + 2 * SUB]
        elif kind == "row":
            src, dst = (row_out.at[1], row_in.at[:, 0]) if dy == 1 else (row_out.at[0], row_in.at[:, 1])
        elif kind == "passed":
            src, dst = pass_out.at[(dx + 1) // 2], pass_in.at[(dx + 1) // 2]
        elif dx == 1:
            src, dst = vel_hbm.at[:, X - 2 : X], ext.at[0:3, 0:2, 0:Y, 0:Z]
        else:
            src, dst = vel_hbm.at[:, 0:2], ext.at[0:3, X + 2 : X + 4, 0:Y, 0:Z]
        copy = pltpu.make_async_remote_copy(
            src_ref=src, dst_ref=dst, send_sem=send_sem.at[m], recv_sem=recv_sem.at[m],
            device_id=device(dx, dy, dz), device_id_type=MESH,
        )
        copies[message] = copy

    def send(message):
        prepare(message)
        guarded(allowed(message[0], message[2])[0], copies[message].start)

    def send_wide(group):
        for message in group:
            prepare(message)

        @pl.when(w == n_wide - 1)
        def _():
            for message in reversed(group):
                copies[message].start()

        @pl.when(w != n_wide - 1)
        def _():
            for message in group:
                copies[message].start()

    def arrive(group):
        for message in group:
            guarded(allowed(message[0], message[2])[1], copies[message].wait_recv)

    send_wide(planes)

    loads[0].wait()
    loads[1].wait()

    lane = lax.broadcasted_iota(jnp.int32, (Y, LANE), 1)
    packed = jnp.zeros((Y, LANE), jnp.float32)
    for x in range(X):
        for c in range(4):
            k = x * 4 + c
            plane = ext[c, x + 2, 0:Y, 0:Z]
            if Z == LANE:
                edge = plane
            else:
                edge = jnp.where(lane < LANE // 2, plane[:, :LANE], plane[:, Z - LANE :])
            moved = pltpu.roll(edge, (4 * k + 2) % LANE, 1)
            packed = jnp.where((lane >= 4 * k) & (lane < 4 * k + 4), moved, packed)
            row_out[0, x, 2 * c : 2 * c + 2] = plane[0:2]
            row_out[1, x, 2 * c : 2 * c + 2] = plane[Y - 2 : Y]
    col_out[...] = packed
    for message in cols + rows:
        send(message)

    for load in loads[2:]:
        load.wait()
    n_blk = seeds_ref.shape[1]
    count = counts_ref[0, 0, 0]
    target = [jnp.where(b < count, dest_ref[0, 0, 0, b], -1) for b in range(n_blk)]
    rank = []
    for b in range(n_blk):
        r = jnp.int32(0)
        for a in range(b):
            r = r + jnp.where(target[a] == target[b], 1, 0)
        rank.append(r)
    for d in range(n_tile):
        for r in range(CAP):
            hits = [jnp.where((target[b] == d) & (rank[b] == r), 1, 0) for b in range(n_blk)]
            for j in range(4):
                line = jnp.zeros((1, LANE), jnp.int32)
                for b in range(n_blk):
                    source = seeds_ref[j, b : b + 1] if j < 3 else steps_ref[b : b + 1]
                    line = line + source * hits[b]
                seed_out[d, 4 * r + j : 4 * r + j + 1] = line
    for message in seeds:
        send(message)
    seed_in[t] = seed_out[t]

    sub8 = lax.broadcasted_iota(jnp.int32, (SUB, LANE), 0)
    lane8 = lax.broadcasted_iota(jnp.int32, (SUB, LANE), 1)
    groups = Y // SUB + 2
    wide_lanes = 32
    per_tile = LANE // wide_lanes
    first_lane = {-1: 0, 1: 16 * (X - 2)}
    near_of = {-1: 0, 1: X - 1}
    far_of = {-1: 1, 1: X - 2}
    lanes_of = [slice(z, z + LANE) for z in range(0, Z, LANE)]
    parts_z = len(lanes_of)
    visc_at = 3 * parts_z
    cols_at = visc_at + parts_z * (Y // SUB)
    col_tiles = -(-groups // per_tile)

    for message in passed:
        dx = message[1]
        n = (dx + 1) // 2
        for z, lanes in enumerate(lanes_of):
            for y in range(Y // SUB):
                pass_out[n, visc_at + z * (Y // SUB) + y] = ext[3, near_of[dx] + 2, y * SUB : (y + 1) * SUB, lanes]
    arrive(cols)
    for message in passed:
        dx = message[1]
        for side in range(len(sides)):
            for tile in range(col_tiles):
                held = jnp.zeros((SUB, LANE), jnp.float32)
                for q in range(min(per_tile, groups - tile * per_tile)):
                    at = (tile * per_tile + q) * SUB
                    group = pltpu.roll(col_in[side, at : at + SUB], (wide_lanes * q - first_lane[dx]) % LANE, 1)
                    held = jnp.where((lane8 >= wide_lanes * q) & (lane8 < wide_lanes * (q + 1)), group, held)
                pass_out[(dx + 1) // 2, cols_at + side * col_tiles + tile] = held
    arrive(rows)
    for message in passed:
        dx = message[1]
        n = (dx + 1) // 2
        near, far = near_of[dx], far_of[dx]
        for z, lanes in enumerate(lanes_of):
            pass_out[n, 3 * z] = row_in[near, 0, :, lanes]
            pass_out[n, 3 * z + 1] = row_in[near, 1, :, lanes]
            for c in range(4):
                pass_out[n, 3 * z + 2, c : c + 1] = row_in[far, 0, 2 * c + 1 : 2 * c + 2, lanes]
                pass_out[n, 3 * z + 2, 4 + c : 5 + c] = row_in[far, 1, 2 * c : 2 * c + 1, lanes]
    send_wide(passed)

    spans = {0: [(x, x + 2) for x in range(X)], 1: [(X - 2, 0), (X - 1, 1)], -1: [(0, X + 2), (1, X + 3)]}
    keep8 = ((sub8 < SUB // 2) & high_open) | ((sub8 >= SUB // 2) & low_open)
    lane_e = lax.broadcasted_iota(jnp.int32, (YE, LANE), 1)

    def unpack(dx):
        n = (dx + 1) // 2
        whole = []
        for side in range(len(sides)):
            if dx == 0:
                parts = [col_in[side, g * SUB : (g + 1) * SUB] for g in range(groups)]
            else:
                parts = [
                    pltpu.roll(
                        pass_in[n, cols_at + side * col_tiles + g // per_tile],
                        (first_lane[dx] - wide_lanes * (g % per_tile)) % LANE, 1,
                    )
                    for g in range(groups)
                ]
            edge = jnp.where(keep8, jnp.where(sub8 < SUB // 2, parts[-1], parts[-2]), 0.0)
            whole.append(jnp.concatenate(parts[:-2] + [edge], 0))
        whole = whole[0] if len(sides) == 1 else jnp.where(lane_e % 4 < 2, whole[0], whole[1])
        for x, here in spans[dx]:
            far = here in (0, X + 3)
            for c in range(3 if far else 4):
                for z, lanes in enumerate(lanes_of):
                    if far:
                        high, low = pass_in[n, 3 * z + 2, 4 + c : 5 + c], pass_in[n, 3 * z + 2, c : c + 1]
                    elif dx == 0:
                        high, low = (row_in[x, side, 2 * c : 2 * c + 2, lanes] for side in (1, 0))
                    else:
                        high, low = (pass_in[n, 3 * z + side, 2 * c : 2 * c + 2] for side in (1, 0))
                    high = jnp.where(high_open, high, 0.0)
                    low = jnp.where(low_open, low, 0.0)
                    gap = jnp.zeros((SUB - 2 * high.shape[0], LANE), jnp.float32)
                    ext[c, here, Y:YE, lanes] = jnp.concatenate([high, gap, low], 0)
                    if c == 3 and dx != 0:
                        for y in range(Y // SUB):
                            ext[c, here, y * SUB : (y + 1) * SUB, lanes] = pass_in[n, visc_at + z * (Y // SUB) + y]
                ext[c, here, :, Z:ZE] = pltpu.roll(whole, LANE - 4 * (x * 4 + c) - 2, 1)

    unpack(0)

    row = lax.broadcasted_iota(jnp.int32, (YE, ZE), 0)
    keep = (row < Y) | ((row < Y + SUB // 2) & high_open) | ((row >= Y + SUB // 2) & low_open)

    def flow(i, carry):
        u = [ext[c, i + 1] for c in range(3)]
        before = [ext[c, i] for c in range(3)]
        after = [ext[c, i + 2] for c in range(3)]
        viscous = ext[3, i + 1]
        up = [[pltpu.roll(u[c], length - 1, axis) for c in range(3)] for axis, length in ((0, YE), (1, ZE))]
        for c in range(3):
            spread = (u[c] + after[c]) * (u[0] + after[0]) - (before[c] + u[c]) * (before[0] + u[0])
            laplace = after[c] + before[c]
            for axis in range(2):
                face = (u[c] + up[axis][c]) * (u[axis + 1] + up[axis][axis + 1])
                spread = spread + (face - pltpu.roll(face, 1, axis))
                laplace = laplace + (up[axis][c] + pltpu.roll(u[c], 1, axis))
            laplace = laplace - 6.0 * u[c]
            fresh = u[c] + flow_step * (viscous * laplace - 0.25 * spread)
            fresh = jnp.where(keep, fresh, 0.0)
            for dz in range(3):
                along = fresh if dz == 1 else pltpu.roll(fresh, 1 if dz == 0 else ZE - 1, 1)
                along = along[:, 0:Z]
                for dy in range(3):
                    moved = along if dy == 1 else pltpu.roll(along, 1 if dy == 0 else YE - 1, 0)
                    shifted[dy, dz, c, i] = moved[0:Y]
        return carry

    lax.fori_loop(2, X, flow, 0)

    def take(dx):
        arrive([message for message in planes + passed if message[1] == dx])
        unpack(dx)

    pl.when(w != 0)(lambda: take(1))
    pl.when(w == 0)(lambda: take(-1))
    base = jnp.where(w == 0, X, 0)
    lax.fori_loop(0, 2, lambda n, carry: flow(base + n, carry), 0)
    pl.when(w != 0)(lambda: take(-1))
    pl.when(w == 0)(lambda: take(1))
    lax.fori_loop(0, 2, lambda n, carry: flow(X - base + n, carry), 0)
    arrive(seeds)
    seed_all[...] = seed_in[...]
    for message in messages:
        guarded(allowed(message[0], message[2])[0], copies[message].wait_send)


def pathlines(shifted, seed_all, new_hbm, out_hbm, dense, out_ref, new_sem, out_sem):
    _, _, _, planes, Y, Z = shifted.shape
    X = planes - 2
    writes = [
        pltpu.make_async_copy(shifted.at[1, 1, c, 1 : X + 1], new_hbm.at[c], new_sem.at[c])
        for c in range(3)
    ]
    for write in writes:
        write.start()

    def hat(e):
        return (jnp.maximum(-e, 0.0), 1.0 - jnp.abs(e), jnp.maximum(e, 0.0))

    def trace(i, carry):
        def sample(e):
            wx, wy, wz = hat(e[0]), hat(e[1]), hat(e[2])
            result = []
            for c in range(3):
                total = None
                for dx in range(3):
                    in_x = None
                    for dy in range(3):
                        in_y = None
                        for dz in range(3):
                            term = wz[dz] * shifted[dy, dz, c, i + dx]
                            in_y = term if in_y is None else in_y + term
                        term = wy[dy] * in_y
                        in_x = term if in_x is None else in_x + term
                    term = wx[dx] * in_x
                    total = term if total is None else total + term
                result.append(total)
            return result

        k1 = [shifted[1, 1, c, i + 1] for c in range(3)]
        k2 = sample([0.5 * trace_step * k for k in k1])
        k3 = sample([0.5 * trace_step * k for k in k2])
        k4 = sample([trace_step * k for k in k3])
        for c in range(3):
            dense[c, i] = trace_step / 6.0 * (k1[c] + 2.0 * k2[c] + 2.0 * k3[c] + k4[c])
        return carry

    lax.fori_loop(0, X, trace, 0)

    sub = lax.broadcasted_iota(jnp.int32, (SUB, LANE), 0)
    for d in range(seed_all.shape[0]):
        for r in range(CAP):
            points = [jnp.broadcast_to(seed_all[d, 4 * r + j : 4 * r + j + 1], (SUB, LANE)) for j in range(4)]
            line = points[0] * Y + points[1]
            for c in range(3):
                found = jnp.zeros((SUB, LANE), jnp.float32)
                for x in range(X):
                    for y in range(0, Y, SUB):
                        for z in range(0, Z, LANE):
                            value = jnp.take_along_axis(
                                dense[c, x, y : y + SUB, z : z + LANE], points[2] & (LANE - 1), axis=1
                            )
                            hit = (line == x * Y + y + sub) & (points[3] > 0)
                            if Z > LANE:
                                hit = hit & (points[2] >= z) & (points[2] < z + LANE)
                            found = jnp.where(hit, value, found)
                slot = d * CAP + r
                out_ref[c, slot : slot + 1] = jnp.sum(found, 0, keepdims=True)
    write = pltpu.make_async_copy(out_ref, out_hbm, out_sem)
    write.start()
    for other in writes:
        other.wait()
    write.wait()


def shards(sizes, velocity, viscosity, counts, destination, seeds, substeps):
    _, X, Y, Z = velocity.shape
    n_wide, n_sec, n_tile = sizes
    n_blk, _, n_pts = seeds.shape[3:]
    sides, cols, rows, planes, passed, seed_msgs = plan(sizes)
    total = len(cols) + len(rows) + len(planes) + len(passed) + len(seed_msgs)
    vmem = pl.BlockSpec(memory_space=pltpu.VMEM)
    hbm = pl.BlockSpec(memory_space=pltpu.HBM)
    f32, i32 = jnp.float32, jnp.int32
    pass_tiles = (Z // LANE) * (3 + Y // SUB) + len(sides) * -(-(Y // SUB + 2) // 4)
    shifted, seed_all = pl.pallas_call(
        functools.partial(exchange, sizes),
        out_shape=(
            jax.ShapeDtypeStruct((3, 3, 3, X + 2, Y, Z), f32),
            jax.ShapeDtypeStruct((n_tile, 4 * CAP, n_pts), i32),
        ),
        in_specs=[pl.BlockSpec(memory_space=pltpu.SMEM)] + [hbm] * 5,
        out_specs=(vmem, vmem),
        scratch_shapes=[
            pltpu.VMEM((4, X + 4, Y + SUB, Z + LANE), f32),
            pltpu.SMEM(destination.shape, i32),
            pltpu.VMEM((3, n_blk, n_pts), i32),
            pltpu.VMEM((n_blk, n_pts), i32),
            pltpu.VMEM((Y, LANE), f32),
            pltpu.VMEM((2, X, SUB, Z), f32),
            pltpu.VMEM((len(sides), Y + 2 * SUB, LANE), f32),
            pltpu.VMEM((X, 2, SUB, Z), f32),
            pltpu.VMEM((2, pass_tiles, SUB, LANE), f32),
            pltpu.VMEM((2, pass_tiles, SUB, LANE), f32),
            pltpu.VMEM((n_tile, 4 * CAP, n_pts), i32),
            pltpu.VMEM((n_tile, 4 * CAP, n_pts), i32),
            pltpu.SemaphoreType.DMA((total,)),
            pltpu.SemaphoreType.DMA((total,)),
            pltpu.SemaphoreType.DMA((5,)),
        ],
        compiler_params=pltpu.CompilerParams(
            collective_id=0, has_side_effects=True, vmem_limit_bytes=16 * 2**20
        ),
    )(
        counts,
        *(pltpu.with_memory_space_constraint(value, pltpu.HBM) for value in (
            destination, velocity, viscosity,
            jnp.transpose(seeds.reshape(n_blk, 3, n_pts), (1, 0, 2)), substeps.reshape(n_blk, n_pts),
        )),
    )
    slots = n_tile * CAP
    fresh, result = pl.pallas_call(
        pathlines,
        out_shape=(
            jax.ShapeDtypeStruct((3, X, Y, Z), f32),
            jax.ShapeDtypeStruct((3, slots, n_pts), f32),
        ),
        in_specs=[vmem, vmem],
        out_specs=(hbm, hbm),
        scratch_shapes=[
            pltpu.VMEM((3, X, Y, Z), f32),
            pltpu.VMEM((3, slots, n_pts), f32),
            pltpu.SemaphoreType.DMA((3,)),
            pltpu.SemaphoreType.DMA,
        ],
        compiler_params=pltpu.CompilerParams(vmem_limit_bytes=16 * 2**20),
    )(shifted, seed_all)
    return fresh, jnp.transpose(result, (1, 0, 2))[None, None, None]


def solution(mesh):
    sizes = tuple(mesh.shape[axis] for axis in ("wide", "sec", "tile"))
    in_specs = (
        P(None, "wide", "tile", "sec"),
        P("wide", "tile", "sec"),
        P("wide", "sec", "tile"),
        P("wide", "sec", "tile", None),
        P("wide", "sec", "tile", None, None, None),
        P("wide", "sec", "tile", None, None),
    )
    out_specs = (P(None, "wide", "tile", "sec"), P("wide", "sec", "tile", None, None, None))
    return jax.shard_map(
        functools.partial(shards, sizes), mesh=mesh, in_specs=in_specs, out_specs=out_specs, check_vma=False
    )
```

```python
import functools

import jax
import jax.numpy as jnp
from jax import lax
from jax.experimental import pallas as pl
from jax.experimental.pallas import tpu as pltpu
from jax.sharding import PartitionSpec as P

CAP = 2
SUB = 8
LANE = 128

flow_step = 0.2
trace_step = 1.25

MESH = pl.DeviceIdType.MESH


def plan(sizes):
    n_wide, n_sec, n_tile = sizes
    sides = (1,) if n_sec == 2 else (1, -1)
    rows = [("row", 0, dy, 0) for dy in (-1, 1)]
    cols = [("col", 0, dy, dz) for dz in sides for dy in (-1, 1, 0)]
    planes = [("plane", dx, 0, 0) for dx in (-1, 1)]
    passed = [("passed", dx, 0, 0) for dx in (-1, 1)]
    seeds = [("seed", 0, dy, 0) for dy in range(1, n_tile)]
    return sides, cols, rows, planes, passed, seeds


def exchange(
    sizes,
    counts_ref, dest_hbm, vel_hbm, visc_hbm, seeds_hbm, steps_hbm,
    new_ref, dense, seed_all,
    ext, shifted, dest_ref, seeds_ref, steps_ref,
    col_out, row_out, col_in, row_in, pass_out, pass_in, seed_out, seed_in,
    send_sem, recv_sem, load_sem,
):
    n_wide, n_sec, n_tile = sizes
    _, X, Y, Z = vel_hbm.shape
    YE, ZE = Y + SUB, Z + LANE
    w, s, t = lax.axis_index("wide"), lax.axis_index("sec"), lax.axis_index("tile")
    sides, cols, rows, planes, passed, seeds = plan(sizes)
    messages = planes + cols + rows + passed + seeds
    low_open = t > 0
    high_open = t < n_tile - 1

    def shift(position, step, size):
        if step % size == 0:
            return position
        moved = position + step % size
        return jnp.where(moved >= size, moved - size, moved)

    w_of = [shift(w, step, n_wide) for step in (0, 1, -1)]
    s_of = [shift(s, step, n_sec) for step in (0, 1, -1)]
    t_of = [shift(t, step, n_tile) for step in range(n_tile)]

    def device(dx, dy, dz):
        return (w_of[dx], s_of[dz], t_of[dy])

    own_vel = ext.at[0:3, 2 : X + 2, 0:Y, 0:Z]
    own_visc = ext.at[3, 2 : X + 2, 0:Y, 0:Z]
    loads = [
        pltpu.make_async_copy(src, dst, load_sem.at[i])
        for i, (src, dst) in enumerate((
            (vel_hbm, own_vel), (visc_hbm, own_visc), (seeds_hbm, seeds_ref),
            (steps_hbm, steps_ref), (dest_hbm, dest_ref),
        ))
    ]
    for load in loads:
        load.start()

    peers = {}
    for _, dx, dy, dz in messages:
        peers.setdefault((dx % n_wide, dy % n_tile, dz % n_sec), (dx, dy, dz))
    barrier = pltpu.get_barrier_semaphore()
    for peer in peers.values():
        pl.semaphore_signal(barrier, inc=1, device_id=device(*peer), device_id_type=MESH)

    pl.semaphore_wait(barrier, len(peers))

    def allowed(kind, dy):
        if kind == "seed" or dy == 0:
            return None, None
        return (high_open, low_open) if dy == 1 else (low_open, high_open)

    def guarded(condition, action):
        if condition is None:
            action()
        else:
            pl.when(condition)(action)

    copies = {}

    def prepare(message):
        kind, dx, dy, dz = message
        m = messages.index(message)
        if kind == "seed":
            src, dst = seed_out.at[t_of[dy]], seed_in.at[t]
        elif kind == "col":
            side = sides.index(dz)
            if dy == 0:
                src, dst = col_out, col_in.at[side, 0:Y]
            elif dy == 1:
                src, dst = col_out.at[Y - SUB : Y], col_in.at[side, Y : Y + SUB]
            else:
                src, dst = col_out.at[0:SUB], col_in.at[side, Y + SUB : Y + 2 * SUB]
        elif kind == "row":
            src, dst = (row_out.at[1], row_in.at[:, 0]) if dy == 1 else (row_out.at[0], row_in.at[:, 1])
        elif kind == "passed":
            src, dst = pass_out.at[(dx + 1) // 2], pass_in.at[(dx + 1) // 2]
        elif dx == 1:
            src, dst = vel_hbm.at[:, X - 2 : X], ext.at[0:3, 0:2, 0:Y, 0:Z]
        else:
            src, dst = vel_hbm.at[:, 0:2], ext.at[0:3, X + 2 : X + 4, 0:Y, 0:Z]
        copy = pltpu.make_async_remote_copy(
            src_ref=src, dst_ref=dst, send_sem=send_sem.at[m], recv_sem=recv_sem.at[m],
            device_id=device(dx, dy, dz), device_id_type=MESH,
        )
        copies[message] = copy

    def send(message):
        prepare(message)
        guarded(allowed(message[0], message[2])[0], copies[message].start)

    def send_wide(group):
        for message in group:
            prepare(message)

        @pl.when(w == n_wide - 1)
        def _():
            for message in reversed(group):
                copies[message].start()

        @pl.when(w != n_wide - 1)
        def _():
            for message in group:
                copies[message].start()

    def arrive(group):
        for message in group:
            guarded(allowed(message[0], message[2])[1], copies[message].wait_recv)

    send_wide(planes)

    loads[0].wait()
    loads[1].wait()

    lane = lax.broadcasted_iota(jnp.int32, (Y, LANE), 1)
    packed = jnp.zeros((Y, LANE), jnp.float32)
    for x in range(X):
        for c in range(4):
            k = x * 4 + c
            plane = ext[c, x + 2, 0:Y, 0:Z]
            if Z == LANE:
                edge = plane
            else:
                edge = jnp.where(lane < LANE // 2, plane[:, :LANE], plane[:, Z - LANE :])
            moved = pltpu.roll(edge, (4 * k + 2) % LANE, 1)
            packed = jnp.where((lane >= 4 * k) & (lane < 4 * k + 4), moved, packed)
            row_out[0, x, 2 * c : 2 * c + 2] = plane[0:2]
            row_out[1, x, 2 * c : 2 * c + 2] = plane[Y - 2 : Y]
    col_out[...] = packed
    for message in cols + rows:
        send(message)

    for load in loads[2:]:
        load.wait()
    n_blk = seeds_ref.shape[1]
    count = counts_ref[0, 0, 0]
    target = [jnp.where(b < count, dest_ref[0, 0, 0, b], -1) for b in range(n_blk)]
    rank = []
    for b in range(n_blk):
        r = jnp.int32(0)
        for a in range(b):
            r = r + jnp.where(target[a] == target[b], 1, 0)
        rank.append(r)
    for d in range(n_tile):
        for r in range(CAP):
            hits = [jnp.where((target[b] == d) & (rank[b] == r), 1, 0) for b in range(n_blk)]
            for j in range(4):
                line = jnp.zeros((1, LANE), jnp.int32)
                for b in range(n_blk):
                    source = seeds_ref[j, b : b + 1] if j < 3 else steps_ref[b : b + 1]
                    line = line + source * hits[b]
                seed_out[d, 4 * r + j : 4 * r + j + 1] = line
    for message in seeds:
        send(message)
    seed_in[t] = seed_out[t]

    sub8 = lax.broadcasted_iota(jnp.int32, (SUB, LANE), 0)
    lane8 = lax.broadcasted_iota(jnp.int32, (SUB, LANE), 1)
    groups = Y // SUB + 2
    wide_lanes = 32
    per_tile = LANE // wide_lanes
    first_lane = {-1: 0, 1: 16 * (X - 2)}
    near_of = {-1: 0, 1: X - 1}
    far_of = {-1: 1, 1: X - 2}
    lanes_of = [slice(z, z + LANE) for z in range(0, Z, LANE)]
    parts_z = len(lanes_of)
    visc_at = 3 * parts_z
    cols_at = visc_at + parts_z * (Y // SUB)
    col_tiles = -(-groups // per_tile)

    for message in passed:
        dx = message[1]
        n = (dx + 1) // 2
        for z, lanes in enumerate(lanes_of):
            for y in range(Y // SUB):
                pass_out[n, visc_at + z * (Y // SUB) + y] = ext[3, near_of[dx] + 2, y * SUB : (y + 1) * SUB, lanes]
    arrive(cols)
    for message in passed:
        dx = message[1]
        for side in range(len(sides)):
            for tile in range(col_tiles):
                held = jnp.zeros((SUB, LANE), jnp.float32)
                for q in range(min(per_tile, groups - tile * per_tile)):
                    at = (tile * per_tile + q) * SUB
                    group = pltpu.roll(col_in[side, at : at + SUB], (wide_lanes * q - first_lane[dx]) % LANE, 1)
                    held = jnp.where((lane8 >= wide_lanes * q) & (lane8 < wide_lanes * (q + 1)), group, held)
                pass_out[(dx + 1) // 2, cols_at + side * col_tiles + tile] = held
    arrive(rows)
    for message in passed:
        dx = message[1]
        n = (dx + 1) // 2
        near, far = near_of[dx], far_of[dx]
        for z, lanes in enumerate(lanes_of):
            pass_out[n, 3 * z] = row_in[near, 0, :, lanes]
            pass_out[n, 3 * z + 1] = row_in[near, 1, :, lanes]
            for c in range(4):
                pass_out[n, 3 * z + 2, c : c + 1] = row_in[far, 0, 2 * c + 1 : 2 * c + 2, lanes]
                pass_out[n, 3 * z + 2, 4 + c : 5 + c] = row_in[far, 1, 2 * c : 2 * c + 1, lanes]
    send_wide(passed)

    spans = {0: [(x, x + 2) for x in range(X)], 1: [(X - 2, 0), (X - 1, 1)], -1: [(0, X + 2), (1, X + 3)]}
    keep8 = ((sub8 < SUB // 2) & high_open) | ((sub8 >= SUB // 2) & low_open)
    lane_e = lax.broadcasted_iota(jnp.int32, (YE, LANE), 1)

    def unpack(dx):
        n = (dx + 1) // 2
        whole = []
        for side in range(len(sides)):
            if dx == 0:
                parts = [col_in[side, g * SUB : (g + 1) * SUB] for g in range(groups)]
            else:
                parts = [
                    pltpu.roll(
                        pass_in[n, cols_at + side * col_tiles + g // per_tile],
                        (first_lane[dx] - wide_lanes * (g % per_tile)) % LANE, 1,
                    )
                    for g in range(groups)
                ]
            edge = jnp.where(keep8, jnp.where(sub8 < SUB // 2, parts[-1], parts[-2]), 0.0)
            whole.append(jnp.concatenate(parts[:-2] + [edge], 0))
        whole = whole[0] if len(sides) == 1 else jnp.where(lane_e % 4 < 2, whole[0], whole[1])
        for x, here in spans[dx]:
            far = here in (0, X + 3)
            for c in range(3 if far else 4):
                for z, lanes in enumerate(lanes_of):
                    if far:
                        high, low = pass_in[n, 3 * z + 2, 4 + c : 5 + c], pass_in[n, 3 * z + 2, c : c + 1]
                    elif dx == 0:
                        high, low = (row_in[x, side, 2 * c : 2 * c + 2, lanes] for side in (1, 0))
                    else:
                        high, low = (pass_in[n, 3 * z + side, 2 * c : 2 * c + 2] for side in (1, 0))
                    high = jnp.where(high_open, high, 0.0)
                    low = jnp.where(low_open, low, 0.0)
                    gap = jnp.zeros((SUB - 2 * high.shape[0], LANE), jnp.float32)
                    ext[c, here, Y:YE, lanes] = jnp.concatenate([high, gap, low], 0)
                    if c == 3 and dx != 0:
                        for y in range(Y // SUB):
                            ext[c, here, y * SUB : (y + 1) * SUB, lanes] = pass_in[n, visc_at + z * (Y // SUB) + y]
                ext[c, here, :, Z:ZE] = pltpu.roll(whole, LANE - 4 * (x * 4 + c) - 2, 1)

    unpack(0)

    row = lax.broadcasted_iota(jnp.int32, (YE, ZE), 0)
    keep = (row < Y) | ((row < Y + SUB // 2) & high_open) | ((row >= Y + SUB // 2) & low_open)

    def flow(i, carry):
        u = [ext[c, i + 1] for c in range(3)]
        before = [ext[c, i] for c in range(3)]
        after = [ext[c, i + 2] for c in range(3)]
        viscous = ext[3, i + 1]
        up = [[pltpu.roll(u[c], length - 1, axis) for c in range(3)] for axis, length in ((0, YE), (1, ZE))]
        for c in range(3):
            spread = (u[c] + after[c]) * (u[0] + after[0]) - (before[c] + u[c]) * (before[0] + u[0])
            laplace = after[c] + before[c]
            for axis in range(2):
                face = (u[c] + up[axis][c]) * (u[axis + 1] + up[axis][axis + 1])
                spread = spread + (face - pltpu.roll(face, 1, axis))
                laplace = laplace + (up[axis][c] + pltpu.roll(u[c], 1, axis))
            laplace = laplace - 6.0 * u[c]
            fresh = u[c] + flow_step * (viscous * laplace - 0.25 * spread)
            fresh = jnp.where(keep, fresh, 0.0)
            for dz in range(3):
                along = fresh if dz == 1 else pltpu.roll(fresh, 1 if dz == 0 else ZE - 1, 1)
                along = along[:, 0:Z]
                for dy in range(3):
                    moved = along if dy == 1 else pltpu.roll(along, 1 if dy == 0 else YE - 1, 0)
                    shifted[dy, dz, c, i] = moved[0:Y]
        return carry

    lax.fori_loop(2, X, flow, 0)

    def hat(e):
        return (jnp.maximum(-e, 0.0), 1.0 - jnp.abs(e), jnp.maximum(e, 0.0))

    def trace(i, carry):
        def sample(e):
            wx, wy, wz = hat(e[0]), hat(e[1]), hat(e[2])
            result = []
            for c in range(3):
                total = None
                for dx in range(3):
                    in_x = None
                    for dy in range(3):
                        in_y = None
                        for dz in range(3):
                            term = wz[dz] * shifted[dy, dz, c, i + dx]
                            in_y = term if in_y is None else in_y + term
                        term = wy[dy] * in_y
                        in_x = term if in_x is None else in_x + term
                    term = wx[dx] * in_x
                    total = term if total is None else total + term
                result.append(total)
            return result

        k1 = [shifted[1, 1, c, i + 1] for c in range(3)]
        k2 = sample([0.5 * trace_step * k for k in k1])
        k3 = sample([0.5 * trace_step * k for k in k2])
        k4 = sample([trace_step * k for k in k3])
        for c in range(3):
            new_ref[c, i] = k1[c]
            dense[c, i] = trace_step / 6.0 * (k1[c] + 2.0 * k2[c] + 2.0 * k3[c] + k4[c])
        return carry

    def take(dx):
        arrive([message for message in planes + passed if message[1] == dx])
        unpack(dx)

    pl.when(w != 0)(lambda: take(1))
    pl.when(w == 0)(lambda: take(-1))
    base = jnp.where(w == 0, X, 0)
    lax.fori_loop(0, 2, lambda n, carry: flow(base + n, carry), 0)
    early = jnp.where(w == 0, 2, 0)
    lax.fori_loop(0, X - 2, lambda n, carry: trace(early + n, carry), 0)
    pl.when(w != 0)(lambda: take(-1))
    pl.when(w == 0)(lambda: take(1))
    lax.fori_loop(0, 2, lambda n, carry: flow(X - base + n, carry), 0)
    late = jnp.where(w == 0, 0, X - 2)
    lax.fori_loop(0, 2, lambda n, carry: trace(late + n, carry), 0)
    arrive(seeds)
    seed_all[...] = seed_in[...]
    for message in messages:
        guarded(allowed(message[0], message[2])[0], copies[message].wait_send)


def lookup(new_ref, dense, seed_all, new_hbm, out_hbm, out_ref, new_sem, out_sem):
    _, X, Y, Z = dense.shape
    new_write = pltpu.make_async_copy(new_ref, new_hbm, new_sem)
    new_write.start()

    sub = lax.broadcasted_iota(jnp.int32, (SUB, LANE), 0)
    for d in range(seed_all.shape[0]):
        for r in range(CAP):
            points = [jnp.broadcast_to(seed_all[d, 4 * r + j : 4 * r + j + 1], (SUB, LANE)) for j in range(4)]
            line = points[0] * Y + points[1]
            for c in range(3):
                found = jnp.zeros((SUB, LANE), jnp.float32)
                for x in range(X):
                    for y in range(0, Y, SUB):
                        for z in range(0, Z, LANE):
                            value = jnp.take_along_axis(
                                dense[c, x, y : y + SUB, z : z + LANE], points[2] & (LANE - 1), axis=1
                            )
                            hit = (line == x * Y + y + sub) & (points[3] > 0)
                            if Z > LANE:
                                hit = hit & (points[2] >= z) & (points[2] < z + LANE)
                            found = jnp.where(hit, value, found)
                slot = d * CAP + r
                out_ref[c, slot : slot + 1] = jnp.sum(found, 0, keepdims=True)
    write = pltpu.make_async_copy(out_ref, out_hbm, out_sem)
    write.start()
    new_write.wait()
    write.wait()


def shards(sizes, velocity, viscosity, counts, destination, seeds, substeps):
    _, X, Y, Z = velocity.shape
    n_wide, n_sec, n_tile = sizes
    n_blk, _, n_pts = seeds.shape[3:]
    sides, cols, rows, planes, passed, seed_msgs = plan(sizes)
    total = len(cols) + len(rows) + len(planes) + len(passed) + len(seed_msgs)
    vmem = pl.BlockSpec(memory_space=pltpu.VMEM)
    hbm = pl.BlockSpec(memory_space=pltpu.HBM)
    f32, i32 = jnp.float32, jnp.int32
    pass_tiles = (Z // LANE) * (3 + Y // SUB) + len(sides) * -(-(Y // SUB + 2) // 4)
    new, dense, seed_all = pl.pallas_call(
        functools.partial(exchange, sizes),
        out_shape=(
            jax.ShapeDtypeStruct((3, X, Y, Z), f32),
            jax.ShapeDtypeStruct((3, X, Y, Z), f32),
            jax.ShapeDtypeStruct((n_tile, 4 * CAP, n_pts), i32),
        ),
        in_specs=[pl.BlockSpec(memory_space=pltpu.SMEM)] + [hbm] * 5,
        out_specs=(vmem, vmem, vmem),
        scratch_shapes=[
            pltpu.VMEM((4, X + 4, Y + SUB, Z + LANE), f32),
            pltpu.VMEM((3, 3, 3, X + 2, Y, Z), f32),
            pltpu.SMEM(destination.shape, i32),
            pltpu.VMEM((3, n_blk, n_pts), i32),
            pltpu.VMEM((n_blk, n_pts), i32),
            pltpu.VMEM((Y, LANE), f32),
            pltpu.VMEM((2, X, SUB, Z), f32),
            pltpu.VMEM((len(sides), Y + 2 * SUB, LANE), f32),
            pltpu.VMEM((X, 2, SUB, Z), f32),
            pltpu.VMEM((2, pass_tiles, SUB, LANE), f32),
            pltpu.VMEM((2, pass_tiles, SUB, LANE), f32),
            pltpu.VMEM((n_tile, 4 * CAP, n_pts), i32),
            pltpu.VMEM((n_tile, 4 * CAP, n_pts), i32),
            pltpu.SemaphoreType.DMA((total,)),
            pltpu.SemaphoreType.DMA((total,)),
            pltpu.SemaphoreType.DMA((5,)),
        ],
        compiler_params=pltpu.CompilerParams(
            collective_id=0, has_side_effects=True, vmem_limit_bytes=16 * 2**20
        ),
    )(
        counts,
        *(pltpu.with_memory_space_constraint(value, pltpu.HBM) for value in (
            destination, velocity, viscosity,
            jnp.transpose(seeds.reshape(n_blk, 3, n_pts), (1, 0, 2)), substeps.reshape(n_blk, n_pts),
        )),
    )
    slots = n_tile * CAP
    fresh, result = pl.pallas_call(
        lookup,
        out_shape=(
            jax.ShapeDtypeStruct((3, X, Y, Z), f32),
            jax.ShapeDtypeStruct((3, slots, n_pts), f32),
        ),
        in_specs=[vmem, vmem, vmem],
        out_specs=(hbm, hbm),
        scratch_shapes=[
            pltpu.VMEM((3, slots, n_pts), f32),
            pltpu.SemaphoreType.DMA,
            pltpu.SemaphoreType.DMA,
        ],
        compiler_params=pltpu.CompilerParams(vmem_limit_bytes=16 * 2**20),
    )(new, dense, seed_all)
    return fresh, jnp.transpose(result, (1, 0, 2))[None, None, None]


def solution(mesh):
    sizes = tuple(mesh.shape[axis] for axis in ("wide", "sec", "tile"))
    in_specs = (
        P(None, "wide", "tile", "sec"),
        P("wide", "tile", "sec"),
        P("wide", "sec", "tile"),
        P("wide", "sec", "tile", None),
        P("wide", "sec", "tile", None, None, None),
        P("wide", "sec", "tile", None, None),
    )
    out_specs = (P(None, "wide", "tile", "sec"), P("wide", "sec", "tile", None, None, None))
    return jax.shard_map(
        functools.partial(shards, sizes), mesh=mesh, in_specs=in_specs, out_specs=out_specs, check_vma=False
    )
```

```python
import functools

import jax
import jax.numpy as jnp
from jax import lax
from jax.experimental import pallas as pl
from jax.experimental.pallas import tpu as pltpu
from jax.sharding import PartitionSpec as P

CAP = 2
SUB = 8
LANE = 128

flow_step = 0.2
trace_step = 1.25

MESH = pl.DeviceIdType.MESH


def plan(sizes):
    n_wide, n_sec, n_tile = sizes
    sides = (1,) if n_sec == 2 else (1, -1)
    rows = [("row", 0, dy, 0) for dy in (-1, 1)]
    cols = [("col", 0, dy, dz) for dz in sides for dy in (-1, 1, 0)]
    planes = [("plane", dx, 0, 0) for dx in (-1, 1)]
    passed = [("passed", dx, 0, 0) for dx in (-1, 1)]
    seeds = [("seed", 0, dy, 0) for dy in range(1, n_tile)]
    return sides, cols, rows, planes, passed, seeds


def exchange(
    sizes,
    counts_ref, dest_hbm, vel_hbm, visc_hbm, seeds_hbm, steps_hbm,
    new_ref, dense, seed_all,
    ext, shifted, dest_ref, seeds_ref, steps_ref,
    col_out, row_out, col_in, row_in, pass_out, pass_in, seed_out, seed_in,
    send_sem, recv_sem, load_sem,
):
    n_wide, n_sec, n_tile = sizes
    _, X, Y, Z = vel_hbm.shape
    YE, ZE = Y + SUB, Z + LANE
    w, s, t = lax.axis_index("wide"), lax.axis_index("sec"), lax.axis_index("tile")
    sides, cols, rows, planes, passed, seeds = plan(sizes)
    messages = planes + cols + rows + passed + seeds
    low_open = t > 0
    high_open = t < n_tile - 1

    def shift(position, step, size):
        if step % size == 0:
            return position
        moved = position + step % size
        return jnp.where(moved >= size, moved - size, moved)

    w_of = [shift(w, step, n_wide) for step in (0, 1, -1)]
    s_of = [shift(s, step, n_sec) for step in (0, 1, -1)]
    t_of = [shift(t, step, n_tile) for step in range(n_tile)]

    def device(dx, dy, dz):
        return (w_of[dx], s_of[dz], t_of[dy])

    own_vel = ext.at[0:3, 2 : X + 2, 0:Y, 0:Z]
    own_visc = ext.at[3, 2 : X + 2, 0:Y, 0:Z]
    loads = [
        pltpu.make_async_copy(src, dst, load_sem.at[i])
        for i, (src, dst) in enumerate((
            (vel_hbm, own_vel), (visc_hbm, own_visc), (seeds_hbm, seeds_ref),
            (steps_hbm, steps_ref), (dest_hbm, dest_ref),
        ))
    ]
    for load in loads:
        load.start()

    peers = {}
    for _, dx, dy, dz in messages:
        peers.setdefault((dx % n_wide, dy % n_tile, dz % n_sec), (dx, dy, dz))
    barrier = pltpu.get_barrier_semaphore()
    for peer in peers.values():
        pl.semaphore_signal(barrier, inc=1, device_id=device(*peer), device_id_type=MESH)

    pl.semaphore_wait(barrier, len(peers))

    def allowed(kind, dy):
        if kind == "seed" or dy == 0:
            return None, None
        return (high_open, low_open) if dy == 1 else (low_open, high_open)

    def guarded(condition, action):
        if condition is None:
            action()
        else:
            pl.when(condition)(action)

    copies = {}

    def prepare(message):
        kind, dx, dy, dz = message
        m = messages.index(message)
        if kind == "seed":
            src, dst = seed_out.at[t_of[dy]], seed_in.at[t]
        elif kind == "col":
            side = sides.index(dz)
            if dy == 0:
                src, dst = col_out, col_in.at[side, 0:Y]
            elif dy == 1:
                src, dst = col_out.at[Y - SUB : Y], col_in.at[side, Y : Y + SUB]
            else:
                src, dst = col_out.at[0:SUB], col_in.at[side, Y + SUB : Y + 2 * SUB]
        elif kind == "row":
            src, dst = (row_out.at[1], row_in.at[:, 0]) if dy == 1 else (row_out.at[0], row_in.at[:, 1])
        elif kind == "passed":
            src, dst = pass_out.at[(dx + 1) // 2], pass_in.at[(dx + 1) // 2]
        elif dx == 1:
            src, dst = vel_hbm.at[:, X - 2 : X], ext.at[0:3, 0:2, 0:Y, 0:Z]
        else:
            src, dst = vel_hbm.at[:, 0:2], ext.at[0:3, X + 2 : X + 4, 0:Y, 0:Z]
        copy = pltpu.make_async_remote_copy(
            src_ref=src, dst_ref=dst, send_sem=send_sem.at[m], recv_sem=recv_sem.at[m],
            device_id=device(dx, dy, dz), device_id_type=MESH,
        )
        copies[message] = copy

    def send(message):
        prepare(message)
        guarded(allowed(message[0], message[2])[0], copies[message].start)

    def send_wide(group):
        for message in group:
            prepare(message)

        @pl.when(w == n_wide - 1)
        def _():
            for message in reversed(group):
                copies[message].start()

        @pl.when(w != n_wide - 1)
        def _():
            for message in group:
                copies[message].start()

    def arrive(group):
        for message in group:
            guarded(allowed(message[0], message[2])[1], copies[message].wait_recv)

    send_wide(planes)

    loads[0].wait()
    loads[1].wait()

    lane = lax.broadcasted_iota(jnp.int32, (Y, LANE), 1)
    packed = jnp.zeros((Y, LANE), jnp.float32)
    for x in range(X):
        for c in range(4):
            k = x * 4 + c
            plane = ext[c, x + 2, 0:Y, 0:Z]
            if Z == LANE:
                edge = plane
            else:
                edge = jnp.where(lane < LANE // 2, plane[:, :LANE], plane[:, Z - LANE :])
            moved = pltpu.roll(edge, (4 * k + 2) % LANE, 1)
            packed = jnp.where((lane >= 4 * k) & (lane < 4 * k + 4), moved, packed)
            row_out[0, x, 2 * c : 2 * c + 2] = plane[0:2]
            row_out[1, x, 2 * c : 2 * c + 2] = plane[Y - 2 : Y]
    col_out[...] = packed
    for message in cols + rows:
        send(message)

    for load in loads[2:]:
        load.wait()
    n_blk = seeds_ref.shape[1]
    count = counts_ref[0, 0, 0]
    target = [jnp.where(b < count, dest_ref[0, 0, 0, b], -1) for b in range(n_blk)]
    rank = []
    for b in range(n_blk):
        r = jnp.int32(0)
        for a in range(b):
            r = r + jnp.where(target[a] == target[b], 1, 0)
        rank.append(r)
    for d in range(n_tile):
        for r in range(CAP):
            hits = [jnp.where((target[b] == d) & (rank[b] == r), 1, 0) for b in range(n_blk)]
            for j in range(4):
                line = jnp.zeros((1, LANE), jnp.int32)
                for b in range(n_blk):
                    source = seeds_ref[j, b : b + 1] if j < 3 else steps_ref[b : b + 1]
                    line = line + source * hits[b]
                seed_out[d, 4 * r + j : 4 * r + j + 1] = line
    for message in seeds:
        send(message)
    seed_in[t] = seed_out[t]

    sub8 = lax.broadcasted_iota(jnp.int32, (SUB, LANE), 0)
    lane8 = lax.broadcasted_iota(jnp.int32, (SUB, LANE), 1)
    groups = Y // SUB + 2
    wide_lanes = 32
    per_tile = LANE // wide_lanes
    first_lane = {-1: 0, 1: 16 * (X - 2)}
    near_of = {-1: 0, 1: X - 1}
    far_of = {-1: 1, 1: X - 2}
    lanes_of = [slice(z, z + LANE) for z in range(0, Z, LANE)]
    parts_z = len(lanes_of)
    visc_at = 3 * parts_z
    cols_at = visc_at + parts_z * (Y // SUB)
    col_tiles = -(-groups // per_tile)

    for message in passed:
        dx = message[1]
        n = (dx + 1) // 2
        for z, lanes in enumerate(lanes_of):
            for y in range(Y // SUB):
                pass_out[n, visc_at + z * (Y // SUB) + y] = ext[3, near_of[dx] + 2, y * SUB : (y + 1) * SUB, lanes]
    arrive(cols)
    for message in passed:
        dx = message[1]
        for side in range(len(sides)):
            for tile in range(col_tiles):
                held = jnp.zeros((SUB, LANE), jnp.float32)
                for q in range(min(per_tile, groups - tile * per_tile)):
                    at = (tile * per_tile + q) * SUB
                    group = pltpu.roll(col_in[side, at : at + SUB], (wide_lanes * q - first_lane[dx]) % LANE, 1)
                    held = jnp.where((lane8 >= wide_lanes * q) & (lane8 < wide_lanes * (q + 1)), group, held)
                pass_out[(dx + 1) // 2, cols_at + side * col_tiles + tile] = held
    arrive(rows)
    for message in passed:
        dx = message[1]
        n = (dx + 1) // 2
        near, far = near_of[dx], far_of[dx]
        for z, lanes in enumerate(lanes_of):
            pass_out[n, 3 * z] = row_in[near, 0, :, lanes]
            pass_out[n, 3 * z + 1] = row_in[near, 1, :, lanes]
            for c in range(4):
                pass_out[n, 3 * z + 2, c : c + 1] = row_in[far, 0, 2 * c + 1 : 2 * c + 2, lanes]
                pass_out[n, 3 * z + 2, 4 + c : 5 + c] = row_in[far, 1, 2 * c : 2 * c + 1, lanes]
    send_wide(passed)

    spans = {0: [(x, x + 2) for x in range(X)], 1: [(X - 2, 0), (X - 1, 1)], -1: [(0, X + 2), (1, X + 3)]}
    keep8 = ((sub8 < SUB // 2) & high_open) | ((sub8 >= SUB // 2) & low_open)
    lane_e = lax.broadcasted_iota(jnp.int32, (YE, LANE), 1)

    def unpack(dx):
        n = (dx + 1) // 2
        whole = []
        for side in range(len(sides)):
            if dx == 0:
                parts = [col_in[side, g * SUB : (g + 1) * SUB] for g in range(groups)]
            else:
                parts = [
                    pltpu.roll(
                        pass_in[n, cols_at + side * col_tiles + g // per_tile],
                        (first_lane[dx] - wide_lanes * (g % per_tile)) % LANE, 1,
                    )
                    for g in range(groups)
                ]
            edge = jnp.where(keep8, jnp.where(sub8 < SUB // 2, parts[-1], parts[-2]), 0.0)
            whole.append(jnp.concatenate(parts[:-2] + [edge], 0))
        whole = whole[0] if len(sides) == 1 else jnp.where(lane_e % 4 < 2, whole[0], whole[1])
        for x, here in spans[dx]:
            far = here in (0, X + 3)
            for c in range(3 if far else 4):
                for z, lanes in enumerate(lanes_of):
                    if far:
                        high, low = pass_in[n, 3 * z + 2, 4 + c : 5 + c], pass_in[n, 3 * z + 2, c : c + 1]
                    elif dx == 0:
                        high, low = (row_in[x, side, 2 * c : 2 * c + 2, lanes] for side in (1, 0))
                    else:
                        high, low = (pass_in[n, 3 * z + side, 2 * c : 2 * c + 2] for side in (1, 0))
                    high = jnp.where(high_open, high, 0.0)
                    low = jnp.where(low_open, low, 0.0)
                    gap = jnp.zeros((SUB - 2 * high.shape[0], LANE), jnp.float32)
                    ext[c, here, Y:YE, lanes] = jnp.concatenate([high, gap, low], 0)
                    if c == 3 and dx != 0:
                        for y in range(Y // SUB):
                            ext[c, here, y * SUB : (y + 1) * SUB, lanes] = pass_in[n, visc_at + z * (Y // SUB) + y]
                ext[c, here, :, Z:ZE] = pltpu.roll(whole, LANE - 4 * (x * 4 + c) - 2, 1)

    unpack(0)

    row = lax.broadcasted_iota(jnp.int32, (YE, ZE), 0)
    keep = (row < Y) | ((row < Y + SUB // 2) & high_open) | ((row >= Y + SUB // 2) & low_open)

    def flow(i, carry):
        u = [ext[c, i + 1] for c in range(3)]
        before = [ext[c, i] for c in range(3)]
        after = [ext[c, i + 2] for c in range(3)]
        viscous = ext[3, i + 1]
        up = [[pltpu.roll(u[c], length - 1, axis) for c in range(3)] for axis, length in ((0, YE), (1, ZE))]
        for c in range(3):
            spread = (u[c] + after[c]) * (u[0] + after[0]) - (before[c] + u[c]) * (before[0] + u[0])
            laplace = after[c] + before[c]
            for axis in range(2):
                face = (u[c] + up[axis][c]) * (u[axis + 1] + up[axis][axis + 1])
                spread = spread + (face - pltpu.roll(face, 1, axis))
                laplace = laplace + (up[axis][c] + pltpu.roll(u[c], 1, axis))
            laplace = laplace - 6.0 * u[c]
            fresh = u[c] + flow_step * (viscous * laplace - 0.25 * spread)
            fresh = jnp.where(keep, fresh, 0.0)
            for dz in range(3):
                along = fresh if dz == 1 else pltpu.roll(fresh, 1 if dz == 0 else ZE - 1, 1)
                along = along[:, 0:Z]
                for dy in range(3):
                    moved = along if dy == 1 else pltpu.roll(along, 1 if dy == 0 else YE - 1, 0)
                    shifted[dy, dz, c, i] = moved[0:Y]
        return carry

    lax.fori_loop(2, X, flow, 0)

    def hat(e):
        return (jnp.maximum(-e, 0.0), 1.0 - jnp.abs(e), jnp.maximum(e, 0.0))

    def trace(i, carry):
        def sample(e):
            wx, wy, wz = hat(e[0]), hat(e[1]), hat(e[2])
            result = []
            for c in range(3):
                total = None
                for dx in range(3):
                    in_x = None
                    for dy in range(3):
                        in_y = None
                        for dz in range(3):
                            term = wz[dz] * shifted[dy, dz, c, i + dx]
                            in_y = term if in_y is None else in_y + term
                        term = wy[dy] * in_y
                        in_x = term if in_x is None else in_x + term
                    term = wx[dx] * in_x
                    total = term if total is None else total + term
                result.append(total)
            return result

        k1 = [shifted[1, 1, c, i + 1] for c in range(3)]
        k2 = sample([0.5 * trace_step * k for k in k1])
        k3 = sample([0.5 * trace_step * k for k in k2])
        k4 = sample([trace_step * k for k in k3])
        for c in range(3):
            new_ref[c, i] = k1[c]
            dense[c, i] = trace_step / 6.0 * (k1[c] + 2.0 * k2[c] + 2.0 * k3[c] + k4[c])
        return carry

    def take(dx):
        arrive([message for message in planes + passed if message[1] == dx])
        unpack(dx)

    high_first = w < n_wide // 2
    pl.when(jnp.logical_not(high_first))(lambda: take(1))
    pl.when(high_first)(lambda: take(-1))
    base = jnp.where(high_first, X, 0)
    lax.fori_loop(0, 2, lambda n, carry: flow(base + n, carry), 0)
    early = jnp.where(high_first, 2, 0)
    lax.fori_loop(0, X - 2, lambda n, carry: trace(early + n, carry), 0)
    pl.when(jnp.logical_not(high_first))(lambda: take(-1))
    pl.when(high_first)(lambda: take(1))
    lax.fori_loop(0, 2, lambda n, carry: flow(X - base + n, carry), 0)
    late = jnp.where(high_first, 0, X - 2)
    lax.fori_loop(0, 2, lambda n, carry: trace(late + n, carry), 0)
    arrive(seeds)
    seed_all[...] = seed_in[...]
    for message in messages:
        guarded(allowed(message[0], message[2])[0], copies[message].wait_send)


def lookup(new_ref, dense, seed_all, new_hbm, out_hbm, out_ref, new_sem, out_sem):
    _, X, Y, Z = dense.shape
    new_write = pltpu.make_async_copy(new_ref, new_hbm, new_sem)
    new_write.start()

    sub = lax.broadcasted_iota(jnp.int32, (SUB, LANE), 0)
    for d in range(seed_all.shape[0]):
        for r in range(CAP):
            points = [jnp.broadcast_to(seed_all[d, 4 * r + j : 4 * r + j + 1], (SUB, LANE)) for j in range(4)]
            line = points[0] * Y + points[1]
            for c in range(3):
                found = jnp.zeros((SUB, LANE), jnp.float32)
                for x in range(X):
                    for y in range(0, Y, SUB):
                        for z in range(0, Z, LANE):
                            value = jnp.take_along_axis(
                                dense[c, x, y : y + SUB, z : z + LANE], points[2] & (LANE - 1), axis=1
                            )
                            hit = (line == x * Y + y + sub) & (points[3] > 0)
                            if Z > LANE:
                                hit = hit & (points[2] >= z) & (points[2] < z + LANE)
                            found = jnp.where(hit, value, found)
                slot = d * CAP + r
                out_ref[c, slot : slot + 1] = jnp.sum(found, 0, keepdims=True)
    write = pltpu.make_async_copy(out_ref, out_hbm, out_sem)
    write.start()
    new_write.wait()
    write.wait()


def shards(sizes, velocity, viscosity, counts, destination, seeds, substeps):
    _, X, Y, Z = velocity.shape
    n_wide, n_sec, n_tile = sizes
    n_blk, _, n_pts = seeds.shape[3:]
    sides, cols, rows, planes, passed, seed_msgs = plan(sizes)
    total = len(cols) + len(rows) + len(planes) + len(passed) + len(seed_msgs)
    vmem = pl.BlockSpec(memory_space=pltpu.VMEM)
    hbm = pl.BlockSpec(memory_space=pltpu.HBM)
    f32, i32 = jnp.float32, jnp.int32
    pass_tiles = (Z // LANE) * (3 + Y // SUB) + len(sides) * -(-(Y // SUB + 2) // 4)
    new, dense, seed_all = pl.pallas_call(
        functools.partial(exchange, sizes),
        out_shape=(
            jax.ShapeDtypeStruct((3, X, Y, Z), f32),
            jax.ShapeDtypeStruct((3, X, Y, Z), f32),
            jax.ShapeDtypeStruct((n_tile, 4 * CAP, n_pts), i32),
        ),
        in_specs=[pl.BlockSpec(memory_space=pltpu.SMEM)] + [hbm] * 5,
        out_specs=(vmem, vmem, vmem),
        scratch_shapes=[
            pltpu.VMEM((4, X + 4, Y + SUB, Z + LANE), f32),
            pltpu.VMEM((3, 3, 3, X + 2, Y, Z), f32),
            pltpu.SMEM(destination.shape, i32),
            pltpu.VMEM((3, n_blk, n_pts), i32),
            pltpu.VMEM((n_blk, n_pts), i32),
            pltpu.VMEM((Y, LANE), f32),
            pltpu.VMEM((2, X, SUB, Z), f32),
            pltpu.VMEM((len(sides), Y + 2 * SUB, LANE), f32),
            pltpu.VMEM((X, 2, SUB, Z), f32),
            pltpu.VMEM((2, pass_tiles, SUB, LANE), f32),
            pltpu.VMEM((2, pass_tiles, SUB, LANE), f32),
            pltpu.VMEM((n_tile, 4 * CAP, n_pts), i32),
            pltpu.VMEM((n_tile, 4 * CAP, n_pts), i32),
            pltpu.SemaphoreType.DMA((total,)),
            pltpu.SemaphoreType.DMA((total,)),
            pltpu.SemaphoreType.DMA((5,)),
        ],
        compiler_params=pltpu.CompilerParams(
            collective_id=0, has_side_effects=True, vmem_limit_bytes=16 * 2**20
        ),
    )(
        counts,
        *(pltpu.with_memory_space_constraint(value, pltpu.HBM) for value in (
            destination, velocity, viscosity,
            jnp.transpose(seeds.reshape(n_blk, 3, n_pts), (1, 0, 2)), substeps.reshape(n_blk, n_pts),
        )),
    )
    slots = n_tile * CAP
    fresh, result = pl.pallas_call(
        lookup,
        out_shape=(
            jax.ShapeDtypeStruct((3, X, Y, Z), f32),
            jax.ShapeDtypeStruct((3, slots, n_pts), f32),
        ),
        in_specs=[vmem, vmem, vmem],
        out_specs=(hbm, hbm),
        scratch_shapes=[
            pltpu.VMEM((3, slots, n_pts), f32),
            pltpu.SemaphoreType.DMA,
            pltpu.SemaphoreType.DMA,
        ],
        compiler_params=pltpu.CompilerParams(vmem_limit_bytes=16 * 2**20),
    )(new, dense, seed_all)
    return fresh, jnp.transpose(result, (1, 0, 2))[None, None, None]


def solution(mesh):
    sizes = tuple(mesh.shape[axis] for axis in ("wide", "sec", "tile"))
    in_specs = (
        P(None, "wide", "tile", "sec"),
        P("wide", "tile", "sec"),
        P("wide", "sec", "tile"),
        P("wide", "sec", "tile", None),
        P("wide", "sec", "tile", None, None, None),
        P("wide", "sec", "tile", None, None),
    )
    out_specs = (P(None, "wide", "tile", "sec"), P("wide", "sec", "tile", None, None, None))
    return jax.shard_map(
        functools.partial(shards, sizes), mesh=mesh, in_specs=in_specs, out_specs=out_specs, check_vma=False
    )
```
